128 devices in a mesh: replica: 4 (over y), fsdp: 32 (over x, z, core).
Axes of the slice: x: 4, y: 4, z: 4, core: 2. Of those that a mesh axis runs over, the one named last changes fastest.
Arguments:
- global_params: float32 [1024, 28672], P(None, 'fsdp'), may hold values from -6 to 6
- local_params: float32 [4, 1024, 28672], P('replica', None, 'fsdp'), may hold values from -6 to 6
- flip_signs: int32 [28672], replicated, may hold values from 0 to 1
- momentum: float32 [1024, 28672], P('fsdp'), may hold values from -6 to 6
- stale_codes: float32 [1024, 28672], P('fsdp'), may hold values from -127 to 127
- stale_scale: float32 [1], replicated, may hold values from 2 to 12
Outputs:
- new_params: float32 [1024, 28672], P(None, 'fsdp')
- new_momentum: float32 [1024, 28672], P('fsdp')
- new_stale: float32 [1024, 28672], P('fsdp')
- new_scale: float32 [1], replicated
The draws below stay inside these ranges and needn't reach their ends.
All inputs are finite; a program needn't handle non-finite values. Where the reference program divides by a largest or mean magnitude, that divisor is 1e-20 or more.
Results may differ from the reference program's by a relative error of at most 0.00008.
Values sent between devices are 32-bit elements; how exact they have to be, the bound alone decides.
A program may use at most 192 MiB of HBM per device.

```python
import math
import jax
import jax.numpy as jnp
from jax import lax

F = 28672
BLOCK = 4096
ROWS = 1024
N_REPLICA = 4


def plant(entries, own_key, least, top_value):
    extent = entries.shape
    spot = [jax.random.randint(jax.random.fold_in(own_key, axis), (), 0, extent[axis]) for axis in range(len(extent))]
    entries = entries.at[tuple(spot)].set(least)
    longest = extent.index(max(extent))
    spot[longest] = (spot[longest] + 1) % extent[longest]
    return entries.at[tuple(spot)].set(top_value)


def shard_levels(key, shape, cuts, least, top_value):
    gain = 1.0
    for axis_at, blocks in cuts:
        draws = jax.random.uniform(jax.random.fold_in(jax.random.fold_in(key, 6), axis_at), (blocks,), jnp.float32, least / len(cuts), top_value / len(cuts))
        gain = gain * jnp.repeat(jnp.exp(draws), shape[axis_at] // blocks).reshape((-1,) + (1,) * (len(shape) - 1 - axis_at))
    return gain


def gaussian(stream_key, shape, spread, bound, shards=(), kind=jnp.bfloat16):
    level = shard_levels(stream_key, shape, shards, -0.22, 0.18) if shards else 1.0
    array = jax.random.normal(stream_key, shape, jnp.float32) * spread * level
    return jnp.minimum(jnp.maximum(array, -bound), bound).astype(kind)


def setup_inputs(seed: int = 0) -> dict:
    seeds = jax.random.split(jax.random.key(seed), 7)
    global_params = gaussian(seeds[0], (ROWS, F), 1.0, 6.0, ((1, 32),), jnp.float32)
    local_params = gaussian(seeds[1], (N_REPLICA, ROWS, F), 1.0, 6.0, ((0, 4), (2, 32)), jnp.float32)
    flip_signs = plant(jax.random.randint(seeds[2], (F,), 0, 2), jax.random.fold_in(seeds[2], 1), 0, 1).astype(jnp.int32)
    momentum = gaussian(seeds[3], (ROWS, F), 1.0, 6.0, ((0, 32),), jnp.float32)
    stale_codes = gaussian(seeds[4], (ROWS, F), 30.0, 127.0, ((0, 32),), jnp.float32)
    stale_scale = jnp.clip(jnp.exp(jax.random.uniform(seeds[5], (1,), jnp.float32, math.log(2.0), math.log(12.0))), 2.0, 12.0)
    return {"global_params": global_params, "local_params": local_params, "flip_signs": flip_signs, "momentum": momentum, "stale_codes": stale_codes, "stale_scale": stale_scale}


def sylvester(order_size):
    indices = jnp.arange(order_size, dtype=jnp.int32)
    common_bits = indices[:, None] & indices[None, :]
    parity = jnp.zeros((order_size, order_size), jnp.int32)
    for bit_index in range(max(order_size.bit_length() - 1, 1)):
        parity = parity + (common_bits >> bit_index & 1)
    return jnp.where(parity % 2 == 0, 1.0, -1.0).astype(jnp.float32)

def rotate(row_block, block_len):
    small_order = block_len // 128
    left_table = sylvester(small_order)
    right_table = sylvester(128)
    row_total, width_total = row_block.shape
    pieces = row_block.reshape(row_total, width_total // block_len, small_order, 128)
    section_one = jnp.einsum('nkab,db->nkad', pieces, right_table, precision=lax.Precision.HIGHEST)
    section_two = jnp.einsum('nkab,ca->nkcb', section_one, left_table, precision=lax.Precision.HIGHEST)
    return (section_two * (1.0 / math.sqrt(block_len))).reshape(row_total, width_total)

def reference(global_params, local_params, flip_signs, momentum, stale_codes, stale_scale):
    flips = (2 * flip_signs - 1).astype(jnp.float32)
    pseudo_grad = global_params[None] - local_params
    rotated = rotate((pseudo_grad * flips).reshape(-1, F), BLOCK)
    new_scale = jnp.max(jnp.abs(rotated)) + 1e-06
    quant_codes = 127.0 * rotated / new_scale
    summed = lax.optimization_barrier(jnp.sum(quant_codes.reshape(N_REPLICA, ROWS, F), axis=0))
    new_stale = summed / N_REPLICA
    mixed = 0.5 * (new_scale / 127.0) * new_stale + 0.5 * (stale_scale[0] / 127.0) * stale_codes
    outer_grad = rotate(mixed, BLOCK) * flips
    new_momentum = 0.9 * momentum + outer_grad
    new_params = global_params - 0.7 * (outer_grad + 0.9 * new_momentum)
    return (new_params, new_momentum, new_stale, new_scale.reshape(1))
```

```python
import functools

import jax
import jax.numpy as jnp
from jax import lax
from jax.experimental import pallas as pl
from jax.experimental.pallas import tpu as pltpu
from jax.sharding import PartitionSpec as P

MESH = pl.DeviceIdType.MESH
F32 = jnp.float32
BF16 = jnp.bfloat16
NF = 32
NR = 4
COLS = 896
FULL = NF * COLS
BLOCK = 4096
NBLK = FULL // BLOCK
PARTS = ((512, 384), (0, 512))
HALF = (pl.ds(0, NF // 2), pl.ds(NF // 2, NF // 2))
ORDER = (4, 12, 1, 3, 5, 15, 7, 13, 8, 2, 9, 6, 11, 14, 10)
PACKED = [sum(v << (4 * i) for i, v in enumerate(ORDER[5 * k : 5 * k + 5])) for k in range(3)]


def fwht(value):
    width = value.shape[1]
    if width == 128:
        return [value]
    left, right = value[:, : width // 2], value[:, width // 2 :]
    return fwht(left + right) + fwht(left - right)


def kernel(
    glob_in, loc_in, flip_in, mom_in, stale_in, sscale_in,
    np_out, nm_out, ns_out, sc_out,
    glob, pg, flips, mom, stale, rot, xrow, npf, table,
    r1a, r1b, r2a, r2b, gqa, gqb, gra, grb, tsend, trecv, nsend, nrecv, mxs, mxr, mys, myr,
    ld_sem, st_sem, lc_sem,
    rs_s, rs_r, sc_s, sc_r, t_s, t_r, gq_s, gq_r, ga_s, ga_r, gb_s, gb_r, ret_s, ret_r, mx_s, mx_r, my_s, my_r,
):
    r, f = lax.axis_index("replica"), lax.axis_index("fsdp")
    fx, fz, fc = f // 8, lax.rem(f // 2, 4), lax.rem(f, 2)
    right, left, far = lax.rem(r + 1, 4), lax.rem(r + 3, 4), lax.rem(r + 2, 4)
    to_right, to_left = (right, f), (left, f)

    def remote(src, dst, ss, rs, dev):
        return pltpu.make_async_remote_copy(
            src_ref=src, dst_ref=dst, send_sem=ss, recv_sem=rs, device_id=dev, device_id_type=MESH
        )

    def lanes(index, width=COLS, off=0):
        return pl.ds(pl.multiple_of(index * COLS + off, 128), width)

    def peers(s, dc):
        word = jnp.where(s < 5, PACKED[0], jnp.where(s < 10, PACKED[1], PACKED[2]))
        code = lax.rem(word >> (4 * lax.rem(s, 5)), 16)
        dx, dz = code // 4, lax.rem(code, 4)
        core = lax.rem(fc + dc, 2)
        to = lax.rem(fx + dx, 4) * 8 + lax.rem(fz + dz, 4) * 2 + core
        frm = lax.rem(fx + 4 - dx, 4) * 8 + lax.rem(fz + 4 - dz, 4) * 2 + core
        return to, frm

    other = f + 1 - 2 * fc

    def each_peer(fn, lo=0, hi=15, core=True):
        def step(s, carry):
            for dc in (0, 1):
                to, frm = peers(s, dc)
                fn(to, frm, 2 * s + dc)
            return carry

        lax.fori_loop(lo, hi, step, 0)
        if core:
            fn(other, other, 30)

    def exchange(src, dst, ss, rs):
        def start(to, frm, i):
            remote(src(to), dst(f), ss.at[i], rs.at[i], (r, to)).start()

        def wait(to, frm, i):
            remote(src(to), dst(frm), ss.at[i], rs.at[i], (r, to)).wait_recv()

        def drain(to, frm, i):
            remote(src(to), dst(f), ss.at[i], rs.at[i], (r, to)).wait_send()

        return start, wait, drain

    order = (far, right, left, r)
    loads = []
    for i, c in enumerate(order):
        a = pltpu.make_async_copy(loc_in.at[:, c], pg.at[:, c], ld_sem.at[2 * i])
        b = pltpu.make_async_copy(glob_in.at[:, c], glob.at[:, c], ld_sem.at[2 * i + 1])
        a.start()
        b.start()
        loads.append((a, b))
    ld_stale = pltpu.make_async_copy(stale_in, stale, ld_sem.at[8])
    ld_mom = pltpu.make_async_copy(mom_in, mom, ld_sem.at[9])
    ld_stale.start()
    ld_mom.start()

    barrier = pltpu.get_barrier_semaphore()

    def greet(s, carry):
        pl.semaphore_signal(
            barrier, inc=1, device_id=(r, lax.rem(f + s, NF)), device_id_type=MESH
        )
        return carry

    lax.fori_loop(1, NF, greet, 0)
    for s in (1, 2, 3):
        pl.semaphore_signal(barrier, inc=1, device_id=(lax.rem(r + s, 4), f), device_id_type=MESH)

    for (a, b), c in zip(loads, order):
        a.wait()
        b.wait()

        def diff(t, carry, c=c):
            rows = pl.ds(4 * t, 4)
            pg[rows, c] = glob[rows, c] - pg[rows, c]
            return carry

        lax.fori_loop(0, NF // 4, diff, 0)
    pl.semaphore_wait(barrier, NF - 1 + NR - 1)

    r1 = ((r1a, r1b)[0], (r1a, r1b)[1])
    r2 = (r2a, r2b)
    gq = (gqa, gqb)
    gr = (gra, grb)

    def cols(p):
        return pl.ds(PARTS[p][0], PARTS[p][1])

    def rs_copies(p):
        lo, hi = HALF
        return (
            remote(pg.at[lo, far, :, cols(p)], r1[p].at[0], rs_s.at[p, 0], rs_r.at[p, 0], to_right),
            remote(pg.at[hi, far, :, cols(p)], r1[p].at[1], rs_s.at[p, 1], rs_r.at[p, 1], to_left),
            remote(pg.at[hi, right, :, cols(p)], r2[p].at[0, hi], rs_s.at[p, 2], rs_r.at[p, 2], to_right),
            remote(pg.at[lo, left, :, cols(p)], r2[p].at[1, lo], rs_s.at[p, 3], rs_r.at[p, 3], to_left),
            remote(r1[p].at[0], r2[p].at[0, lo], rs_s.at[p, 4], rs_r.at[p, 4], to_right),
            remote(r1[p].at[1], r2[p].at[1, hi], rs_s.at[p, 5], rs_r.at[p, 5], to_left),
        )

    rs = (rs_copies(0), rs_copies(1))

    def rs_first(p):
        for i in range(4):
            rs[p][i].start()

    def rs_second(p):
        for side, c, base in ((0, right, 0), (1, left, NF // 2)):
            rs[p][side].wait_recv()

            def add(t, carry, side=side, c=c, base=base):
                rows = pl.ds(4 * t, 4)
                r1[p][side, rows] = r1[p][side, rows] + pg[pl.ds(base + 4 * t, 4), c, :, cols(p)]
                return carry

            lax.fori_loop(0, NF // 8, add, 0)
            rs[p][4 + side].start()

    def rs_last(p):
        for i in range(2, 6):
            rs[p][i].wait_recv()

        def add(t, carry):
            rows = pl.ds(4 * t, 4)
            gq[p][rows] = pg[rows, r, :, cols(p)] + (r2[p][0, rows] + r2[p][1, rows])
            return carry

        lax.fori_loop(0, NF // 4, add, 0)

    rs_first(0)

    sc_start, sc_wait, sc_drain = exchange(
        lambda to: pg.at[to], lambda frm: xrow.at[:, :, lanes(frm)], sc_s, sc_r
    )
    each_peer(sc_start, 0, 5, True)
    for i in range(NR):
        xrow[i, :, lanes(f)] = pg[f, i]

    flips[...] = jnp.broadcast_to((2 * flip_in[...] - 1).astype(F32), (8, FULL))
    bits = lax.broadcasted_iota(jnp.int32, (256, 128), 0) & lax.broadcasted_iota(jnp.int32, (256, 128), 1)
    parity = jnp.zeros((256, 128), jnp.int32)
    for b in range(7):
        parity = parity ^ (bits >> b)
    table[...] = jnp.where((parity & 1) == 0, 1.0 / 64.0, -1.0 / 64.0).astype(F32).astype(BF16)

    def hadamard(value):
        x = jnp.concatenate(fwht(value), axis=0)
        high = x.astype(BF16)
        low = (x - high.astype(F32)).astype(BF16)
        return jnp.dot(
            jnp.concatenate([high, low], axis=1), table[...], preferred_element_type=F32
        )

    def to_rows(value):
        return jnp.concatenate([value[8 * a : 8 * a + 8] for a in range(32)], axis=1)

    def blk(k):
        return pl.ds(pl.multiple_of(k * BLOCK, BLOCK), BLOCK)

    coef = 0.5 * (sscale_in[0] / 127.0)
    ld_stale.wait()

    def stale_step(t, carry):
        i, k = t // NBLK, lax.rem(t, NBLK)
        stale[i, :, blk(k)] = to_rows(hadamard(stale[i, :, blk(k)])) * (flips[:, blk(k)] * coef)
        return carry

    lax.fori_loop(0, NR * NBLK, stale_step, 0)
    ld_mom.wait()
    off1, wid1 = PARTS[1]
    off0, wid0 = PARTS[0]

    def t_step(g, carry):
        tsend[g] = 1.9 * stale[r, :, lanes(g, wid1, off1)] + 0.81 * mom[r, :, lanes(g, wid1, off1)]
        return carry

    lax.fori_loop(0, NF, t_step, 0)
    t_start, t_wait, t_drain = exchange(
        lambda to: tsend.at[to], lambda frm: trecv.at[frm], t_s, t_r
    )
    each_peer(t_start)
    trecv[f] = tsend[f]

    rs_second(0)
    rs_first(1)

    def gq_ops(p):
        return exchange(
            lambda to: gq[p].at[to], lambda frm: gr[p].at[r, frm], gq_s.at[p], gq_r.at[p]
        )

    gq0, gq1 = gq_ops(0), gq_ops(1)

    def gather(ref, lo, hi, ss, sr):
        del lo, hi
        return (
            remote(ref(r, 0), ref(r, 0), ss.at[0], sr.at[0], to_right),
            remote(ref(r, 1), ref(r, 1), ss.at[1], sr.at[1], to_left),
            remote(ref(r, 1), ref(r, 1), ss.at[2], sr.at[2], to_right),
            remote(ref(r, 0), ref(r, 0), ss.at[3], sr.at[3], to_left),
            remote(ref(left, 0), ref(left, 0), ss.at[4], sr.at[4], to_right),
            remote(ref(right, 1), ref(right, 1), ss.at[5], sr.at[5], to_left),
        )

    ga = [
        gather(lambda c, h, p=p: gr[p].at[c, HALF[h]], 0, 0, ga_s.at[p], ga_r.at[p]) for p in (0, 1)
    ]
    gb = gather(lambda c, h: npf.at[HALF[h], c, :, cols(1)], 0, 0, gb_s, gb_r)

    def gather_start(g):
        for i in range(4):
            g[i].start()

    def gather_forward(g):
        for i in range(2):
            g[i].wait_recv()
            g[4 + i].start()

    rs_last(0)
    each_peer(gq0[0])
    gra[r, f] = gqa[f]
    each_peer(sc_start, 5, 10, False)

    rs_second(1)
    each_peer(gq0[1])
    gather_start(ga[0])

    rs_last(1)
    each_peer(gq1[0])
    grb[r, f] = gqb[f]
    each_peer(t_wait)

    def np_step(t, carry):
        rows = pl.ds(4 * t, 4)
        npf[rows, r, :, cols(1)] = glob[rows, r, :, cols(1)] - 0.7 * (trecv[rows] + 0.2375 * gqb[rows])
        return carry

    lax.fori_loop(0, NF // 4, np_step, 0)
    gather_start(gb)
    each_peer(sc_start, 10, 15, False)

    gather_forward(ga[0])
    each_peer(gq1[1])
    gather_start(ga[1])
    gather_forward(gb)

    for i in range(2, 6):
        ga[0][i].wait_recv()

    def n_step(t, carry):
        i, g = t // NF, lax.rem(t, NF)
        nsend[g, i] = (
            1.9 * (0.125 * gra[i, g] + stale[i, :, lanes(g, wid0, off0)])
            + 0.81 * mom[i, :, lanes(g, wid0, off0)]
        )
        return carry

    lax.fori_loop(0, NR * NF, n_step, 0)
    ret_start, ret_wait, ret_drain = exchange(
        lambda to: nsend.at[to], lambda frm: nrecv.at[frm], ret_s, ret_r
    )
    each_peer(ret_start)
    nrecv[f] = nsend[f]

    each_peer(sc_wait)

    def scale_step(t, top):
        i, k = t // NBLK, lax.rem(t, NBLK)
        y = jnp.abs(hadamard(xrow[i, :, blk(k)] * flips[:, blk(k)]))
        return jnp.maximum(top, jnp.max(y.reshape(32, 8, 128), axis=0))

    mxs[...] = lax.fori_loop(0, NR * NBLK, scale_step, jnp.zeros((8, 128), F32))
    mx_start, mx_wait, mx_drain = exchange(lambda to: mxs, lambda frm: mxr.at[frm], mx_s, mx_r)
    each_peer(mx_start)
    mxr[f] = mxs[...]

    gather_forward(ga[1])

    def rows_of(i):
        def mom_step(g, carry):
            for p, (off, wid) in enumerate(PARTS):
                at = lanes(g, wid, off)
                v = gr[p][i, g]
                mom[i, :, at] = 0.9 * mom[i, :, at] + (0.125 * v + stale[i, :, at])
                rot[i, :, at] = v * flips[:, at]
            return carry

        lax.fori_loop(0, NF, mom_step, 0)
        pltpu.make_async_copy(mom.at[i], nm_out.at[i], st_sem.at[i]).start()

        def rot_step(k, carry):
            rot[i, :, blk(k)] = to_rows(hadamard(rot[i, :, blk(k)]))
            return carry

        lax.fori_loop(0, NBLK, rot_step, 0)

    rows_of(r)

    each_peer(mx_wait)
    mys[...] = jnp.max(mxr[...], axis=0)

    def my_copy(s):
        return remote(
            mys, myr.at[s - 1], my_s.at[s - 1], my_r.at[s - 1], (lax.rem(r + s, 4), f)
        )

    for s in (1, 2, 3):
        my_copy(s).start()

    ga[1][3].wait_recv()
    rows_of(right)
    ga[1][2].wait_recv()
    rows_of(left)

    for s in (1, 2, 3):
        my_copy(s).wait_recv()
    top = jnp.maximum(jnp.max(myr[...], axis=0), mys[...])
    scale = jnp.max(top) + 1e-06
    sc_out[0] = scale
    factor = 31.75 / jnp.broadcast_to(scale, (8, 128))

    each_peer(ret_wait)

    def np0_step(t, carry):
        npf[t, :, :, cols(0)] = glob[t, :, :, cols(0)] - 0.7 * nrecv[t]
        return carry

    lax.fori_loop(0, NF, np0_step, 0)
    for i in range(2, 6):
        gb[i].wait_recv()
    st_np = pltpu.make_async_copy(npf, np_out, st_sem.at[8])
    st_np.start()

    def finish(i):
        def fin_step(t, carry):
            at = pl.ds(pl.multiple_of(t * COLS, 128), COLS)
            rot[i, :, at] = rot[i, :, at] * jnp.concatenate([factor] * 7, axis=1)
            return carry

        lax.fori_loop(0, NF, fin_step, 0)
        pltpu.make_async_copy(rot.at[i], ns_out.at[i], st_sem.at[4 + i]).start()

    finish(r)
    finish(right)
    finish(left)
    for i in (4, 5):
        ga[1][i].wait_recv()
    rows_of(far)
    finish(far)

    for p in (0, 1):
        for c in rs[p]:
            c.wait_send()
        for c in ga[p]:
            c.wait_send()
    for c in gb:
        c.wait_send()
    for d in (sc_drain, t_drain, gq0[2], gq1[2], ret_drain, mx_drain):
        each_peer(d)
    for s in (1, 2, 3):
        my_copy(s).wait_send()
    for i in range(NR):
        pltpu.make_async_copy(mom.at[i], nm_out.at[i], st_sem.at[i]).wait()
        pltpu.make_async_copy(rot.at[i], ns_out.at[i], st_sem.at[4 + i]).wait()
    st_np.wait()


def body(global_params, local_params, flip_signs, momentum, stale_codes, stale_scale):
    shape = jax.ShapeDtypeStruct
    hbm = pl.BlockSpec(memory_space=pl.ANY)
    vmem = pl.BlockSpec(memory_space=pltpu.VMEM)
    smem = pl.BlockSpec(memory_space=pltpu.SMEM)
    dma = pltpu.SemaphoreType.DMA
    w0, w1 = PARTS[0][1], PARTS[1][1]
    col4, row4 = (NF, NR, 8, COLS), (NR, 8, FULL)

    def buf(*dims):
        return pltpu.VMEM(dims, F32)

    new_params, new_momentum, new_stale, new_scale = pl.pallas_call(
        kernel,
        out_shape=(shape(col4, F32), shape(row4, F32), shape(row4, F32), shape((1,), F32)),
        in_specs=[hbm, hbm, vmem, hbm, hbm, smem],
        out_specs=(hbm, hbm, hbm, smem),
        scratch_shapes=[
            buf(*col4), buf(*col4), buf(8, FULL), buf(*row4), buf(*row4), buf(*row4), buf(*row4), buf(*col4),
            pltpu.VMEM((256, 128), BF16),
            buf(2, NF // 2, 8, w0), buf(2, NF // 2, 8, w1), buf(2, NF, 8, w0), buf(2, NF, 8, w1),
            buf(NF, 8, w0), buf(NF, 8, w1), buf(NR, NF, 8, w0), buf(NR, NF, 8, w1),
            buf(NF, 8, w1), buf(NF, 8, w1), buf(NF, NR, 8, w0), buf(NF, NR, 8, w0),
            buf(8, 128), buf(NF, 8, 128), buf(8, 128), buf(3, 8, 128),
            dma((10,)), dma((9,)), dma((1,)),
            dma((2, 6)), dma((2, 6)), dma((31,)), dma((31,)), dma((31,)), dma((31,)),
            dma((2, 31)), dma((2, 31)), dma((2, 6)), dma((2, 6)), dma((6,)), dma((6,)),
            dma((31,)), dma((31,)), dma((31,)), dma((31,)), dma((3,)), dma((3,)),
        ],
        compiler_params=pltpu.CompilerParams(
            collective_id=0, has_side_effects=True, vmem_limit_bytes=48 * 2**20
        ),
        name="outer_step",
    )(
        global_params.reshape(col4), local_params.reshape(col4), flip_signs.reshape(1, FULL),
        momentum.reshape(row4), stale_codes.reshape(row4), stale_scale,
    )
    return (
        new_params.reshape(NF * NR * 8, COLS),
        new_momentum.reshape(NR * 8, FULL),
        new_stale.reshape(NR * 8, FULL),
        new_scale,
    )


def solution(mesh):
    placed = (
        P(None, "fsdp"),
        P("replica", None, "fsdp"),
        P(),
        P("fsdp", None),
        P("fsdp", None),
        P(),
    )
    return jax.shard_map(
        body,
        mesh=mesh,
        in_specs=placed,
        out_specs=(P(None, "fsdp"), P("fsdp", None), P("fsdp", None), P()),
        check_vma=False,
    )
```

```python
import jax
import jax.numpy as jnp
from jax import lax
from jax.experimental import pallas as pl
from jax.experimental.pallas import tpu as pltpu
from jax.sharding import PartitionSpec as P

MESH = pl.DeviceIdType.MESH
F32 = jnp.float32
BF16 = jnp.bfloat16
NF = 32
NR = 4
COLS = 896
FULL = NF * COLS
BLOCK = 4096
NBLK = FULL // BLOCK
PARTS = ((640, 256), (0, 640))
CUTS = (5, 10)
HALF = (pl.ds(0, NF // 2), pl.ds(NF // 2, NF // 2))
ORDER = (4, 12, 1, 3, 5, 15, 7, 13, 8, 2, 9, 6, 11, 14, 10)
PACKED = [sum(v << (4 * i) for i, v in enumerate(ORDER[5 * k : 5 * k + 5])) for k in range(3)]


def fwht(value):
    width = value.shape[1]
    if width == 128:
        return [value]
    left, right = value[:, : width // 2], value[:, width // 2 :]
    return fwht(left + right) + fwht(left - right)


def kernel(
    glob_in, loc_in, flip_in, mom_in, stale_in, sscale_in,
    npf, mom, rot, top_out,
    glob, pg, signs, flips, stale, xrow, table,
    r1a, r1b, r2a, r2b, gqa, gqb, gra, grb, tsend, trecv, nsend, nrecv, mxs, mxr, mys, myr,
    ld_sem,
    rs_s, rs_r, sc_s, sc_r, t_s, t_r, gq_s, gq_r, ga_s, ga_r, gb_s, gb_r, ret_s, ret_r, mx_s, mx_r, my_s, my_r,
):
    r, f = lax.axis_index("replica"), lax.axis_index("fsdp")
    fx, fz, fc = f // 8, lax.rem(f // 2, 4), lax.rem(f, 2)
    right, left, far = lax.rem(r + 1, 4), lax.rem(r + 3, 4), lax.rem(r + 2, 4)
    to_right, to_left = (right, f), (left, f)

    def remote(src, dst, ss, rs, dev):
        return pltpu.make_async_remote_copy(
            src_ref=src, dst_ref=dst, send_sem=ss, recv_sem=rs, device_id=dev, device_id_type=MESH
        )

    def lanes(index, width=COLS, off=0):
        return pl.ds(pl.multiple_of(index * COLS + off, 128), width)

    def peers(s, dc):
        word = jnp.where(s < 5, PACKED[0], jnp.where(s < 10, PACKED[1], PACKED[2]))
        code = lax.rem(word >> (4 * lax.rem(s, 5)), 16)
        dx, dz = code // 4, lax.rem(code, 4)
        core = lax.rem(fc + dc, 2)
        to = lax.rem(fx + dx, 4) * 8 + lax.rem(fz + dz, 4) * 2 + core
        frm = lax.rem(fx + 4 - dx, 4) * 8 + lax.rem(fz + 4 - dz, 4) * 2 + core
        return to, frm

    other = f + 1 - 2 * fc

    def each_peer(fn, lo=0, hi=15, core=True):
        def step(s, carry):
            for dc in (0, 1):
                to, frm = peers(s, dc)
                fn(to, frm, 2 * s + dc)
            return carry

        lax.fori_loop(lo, hi, step, 0)
        if core:
            fn(other, other, 30)

    def exchange(src, dst, ss, rs, all_src, all_dst):
        def start(to, frm, i):
            remote(src(to), dst(f), ss, rs, (r, to)).start()

        def wait():
            remote(all_src, all_dst, ss, rs, (r, other)).wait_recv()

        def drain():
            remote(all_src, all_dst, ss, rs, (r, other)).wait_send()

        return start, wait, drain

    most = pl.ds(0, NF - 1)

    order = (far, right, left, r)
    loads = []
    for i, c in enumerate(order):
        a = pltpu.make_async_copy(loc_in.at[:, c], pg.at[:, c], ld_sem.at[2 * i])
        b = pltpu.make_async_copy(glob_in.at[:, c], glob.at[:, c], ld_sem.at[2 * i + 1])
        a.start()
        b.start()
        loads.append((a, b))
    ld_stale = pltpu.make_async_copy(stale_in, stale, ld_sem.at[8])
    ld_mom = pltpu.make_async_copy(mom_in, mom, ld_sem.at[9])
    ld_signs = pltpu.make_async_copy(flip_in, signs, ld_sem.at[10])
    ld_signs.start()
    ld_stale.start()
    ld_mom.start()

    barrier = pltpu.get_barrier_semaphore()

    def greet(s, carry):
        pl.semaphore_signal(
            barrier, inc=1, device_id=(r, lax.rem(f + s, NF)), device_id_type=MESH
        )
        return carry

    lax.fori_loop(1, NF, greet, 0)
    for s in (1, 2, 3):
        pl.semaphore_signal(barrier, inc=1, device_id=(lax.rem(r + s, 4), f), device_id_type=MESH)

    def difference(i):
        c = order[i]
        for load in loads[i]:
            load.wait()

        def diff(t, carry):
            rows = pl.ds(4 * t, 4)
            pg[rows, c] = glob[rows, c] - pg[rows, c]
            return carry

        lax.fori_loop(0, NF // 4, diff, 0, unroll=2)

    difference(0)
    pl.semaphore_wait(barrier, NF - 1 + NR - 1)

    r1 = (r1a, r1b)
    r2 = (r2a, r2b)
    gq = (gqa, gqb)
    gr = (gra, grb)

    def cols(p):
        return pl.ds(PARTS[p][0], PARTS[p][1])

    def rs_copies(p):
        lo, hi = HALF
        return (
            remote(pg.at[lo, far, :, cols(p)], r1[p].at[0], rs_s.at[p, 0], rs_r.at[p, 0], to_right),
            remote(pg.at[hi, far, :, cols(p)], r1[p].at[1], rs_s.at[p, 1], rs_r.at[p, 1], to_left),
            remote(pg.at[hi, right, :, cols(p)], r2[p].at[0, hi], rs_s.at[p, 2], rs_r.at[p, 2], to_right),
            remote(pg.at[lo, left, :, cols(p)], r2[p].at[1, lo], rs_s.at[p, 3], rs_r.at[p, 3], to_left),
            remote(r1[p].at[0], r2[p].at[0, lo], rs_s.at[p, 4], rs_r.at[p, 4], to_right),
            remote(r1[p].at[1], r2[p].at[1, hi], rs_s.at[p, 5], rs_r.at[p, 5], to_left),
        )

    rs = (rs_copies(0), rs_copies(1))

    def rs_second(p):
        for side, c, base in ((0, right, 0), (1, left, NF // 2)):
            rs[p][side].wait_recv()

            def add(t, carry, side=side, c=c, base=base):
                rows = pl.ds(4 * t, 4)
                r1[p][side, rows] = r1[p][side, rows] + pg[pl.ds(base + 4 * t, 4), c, :, cols(p)]
                return carry

            lax.fori_loop(0, NF // 8, add, 0, unroll=2)
            rs[p][4 + side].start()

    def rs_last(p):
        for i in range(2, 6):
            rs[p][i].wait_recv()

        def add(t, carry):
            rows = pl.ds(4 * t, 4)
            gq[p][rows] = pg[rows, r, :, cols(p)] + (r2[p][0, rows] + r2[p][1, rows])
            return carry

        lax.fori_loop(0, NF // 4, add, 0, unroll=2)

    for i in (0, 1):
        rs[0][i].start()
    difference(1)
    difference(2)
    for i in (2, 3):
        rs[0][i].start()
    for i in (0, 1):
        rs[1][i].start()
    difference(3)

    sc_start, sc_wait, sc_drain = exchange(
        lambda to: pg.at[to], lambda frm: xrow.at[:, :, lanes(frm)], sc_s.at[0], sc_r.at[0],
        pg.at[most], xrow.at[:, :, pl.ds(0, (NF - 1) * COLS)],
    )
    each_peer(sc_start, 0, CUTS[0], True)
    for i in range(NR):
        xrow[i, :, lanes(f)] = pg[f, i]

    rs_second(0)
    for i in (2, 3):
        rs[1][i].start()

    ld_signs.wait()

    def flip_step(t, carry):
        rows = (2 * signs[pl.ds(8 * t, 8), :] - 1).astype(F32)
        flips[:, pl.ds(pl.multiple_of(t * 1024, 1024), 1024)] = jnp.concatenate(
            [jnp.broadcast_to(rows[i : i + 1], (8, 128)) for i in range(8)], axis=1
        )
        return carry

    lax.fori_loop(0, FULL // 1024, flip_step, 0, unroll=2)
    bits = lax.broadcasted_iota(jnp.int32, (256, 128), 0) & lax.broadcasted_iota(jnp.int32, (256, 128), 1)
    parity = jnp.zeros((256, 128), jnp.int32)
    for b in range(7):
        parity = parity ^ (bits >> b)
    table[...] = jnp.where((parity & 1) == 0, 1.0 / 64.0, -1.0 / 64.0).astype(F32).astype(BF16)

    def hadamard(value):
        x = jnp.concatenate(fwht(value), axis=0)
        high = x.astype(BF16)
        low = (x - high.astype(F32)).astype(BF16)
        return jnp.dot(
            jnp.concatenate([high, low], axis=1), table[...], preferred_element_type=F32
        )

    def to_rows(value):
        return jnp.concatenate([value[8 * a : 8 * a + 8] for a in range(32)], axis=1)

    def blk(k):
        return pl.ds(pl.multiple_of(k * BLOCK, BLOCK), BLOCK)

    coef = 0.5 * (sscale_in[0] / 127.0)
    ld_stale.wait()

    def stale_step(t, carry):
        i, k = t // NBLK, lax.rem(t, NBLK)
        stale[i, :, blk(k)] = to_rows(hadamard(stale[i, :, blk(k)])) * (flips[:, blk(k)] * coef)
        return carry

    lax.fori_loop(0, NR * NBLK, stale_step, 0, unroll=4)
    ld_mom.wait()
    off1, wid1 = PARTS[1]
    off0, wid0 = PARTS[0]

    def t_step(g, carry):
        tsend[g] = 1.9 * stale[r, :, lanes(g, wid1, off1)] + 0.81 * mom[r, :, lanes(g, wid1, off1)]
        return carry

    lax.fori_loop(0, NF, t_step, 0, unroll=4)
    t_start, t_wait, t_drain = exchange(
        lambda to: tsend.at[to], lambda frm: trecv.at[frm], t_s.at[0], t_r.at[0],
        tsend.at[most], trecv.at[most],
    )
    each_peer(t_start)
    trecv[f] = tsend[f]

    def gq_ops(p):
        return exchange(
            lambda to: gq[p].at[to], lambda frm: gr[p].at[r, frm], gq_s.at[p], gq_r.at[p],
            gq[p].at[most], gr[p].at[r, most],
        )

    gq0, gq1 = gq_ops(0), gq_ops(1)

    def gather(ref, ss, sr):
        return (
            remote(ref(r, 0), ref(r, 0), ss.at[0], sr.at[0], to_right),
            remote(ref(r, 1), ref(r, 1), ss.at[1], sr.at[1], to_left),
            remote(ref(r, 1), ref(r, 1), ss.at[2], sr.at[2], to_right),
            remote(ref(r, 0), ref(r, 0), ss.at[3], sr.at[3], to_left),
            remote(ref(left, 0), ref(left, 0), ss.at[4], sr.at[4], to_right),
            remote(ref(right, 1), ref(right, 1), ss.at[5], sr.at[5], to_left),
        )

    ga = [
        gather(lambda c, h, p=p: gr[p].at[c, HALF[h]], ga_s.at[p], ga_r.at[p]) for p in (0, 1)
    ]
    gb = gather(lambda c, h: npf.at[HALF[h], c, :, cols(1)], gb_s, gb_r)

    def gather_start(g):
        for i in range(4):
            g[i].start()

    def gather_forward(g):
        for i in range(2):
            g[i].wait_recv()
            g[4 + i].start()

    def rows_of(i):
        def mom_step(g, carry):
            for p, (off, wid) in enumerate(PARTS):
                at = lanes(g, wid, off)
                v = gr[p][i, g]
                mom[i, :, at] = 0.9 * mom[i, :, at] + (0.125 * v + stale[i, :, at])
                rot[i, :, at] = v * flips[:, at]
            return carry

        lax.fori_loop(0, NF, mom_step, 0, unroll=4)

        def rot_step(k, carry):
            rot[i, :, blk(k)] = to_rows(hadamard(rot[i, :, blk(k)]))
            return carry

        lax.fori_loop(0, NBLK, rot_step, 0, unroll=NBLK)

    rs_last(0)
    each_peer(gq0[0])
    gra[r, f] = gqa[f]
    each_peer(sc_start, CUTS[0], CUTS[1], False)
    rs_second(1)
    gq0[1]()
    gather_start(ga[0])

    rs_last(1)
    each_peer(gq1[0])
    each_peer(sc_start, CUTS[1], 15, False)
    grb[r, f] = gqb[f]
    t_wait()

    def np_step(t, carry):
        rows = pl.ds(4 * t, 4)
        npf[rows, r, :, cols(1)] = glob[rows, r, :, cols(1)] - 0.7 * (trecv[rows] + 0.2375 * gqb[rows])
        return carry

    lax.fori_loop(0, NF // 4, np_step, 0, unroll=2)
    gather_start(gb)
    gather_forward(ga[0])
    gq1[1]()
    gather_start(ga[1])

    for i in range(2, 6):
        ga[0][i].wait_recv()

    def n_step(t, carry):
        i, g = t // NF, lax.rem(t, NF)
        nsend[g, i] = (
            1.9 * (0.125 * gra[i, g] + stale[i, :, lanes(g, wid0, off0)])
            + 0.81 * mom[i, :, lanes(g, wid0, off0)]
        )
        return carry

    lax.fori_loop(0, NR * NF, n_step, 0, unroll=4)
    ret_start, ret_wait, ret_drain = exchange(
        lambda to: nsend.at[to], lambda frm: nrecv.at[frm], ret_s.at[0], ret_r.at[0],
        nsend.at[most], nrecv.at[most],
    )
    each_peer(ret_start)
    nrecv[f] = nsend[f]

    rows_of(r)
    gather_forward(ga[1])
    gather_forward(gb)

    sc_wait()

    def scale_step(t, top):
        i, k = t // NBLK, lax.rem(t, NBLK)
        y = jnp.abs(hadamard(xrow[i, :, blk(k)] * flips[:, blk(k)]))
        return jnp.maximum(top, jnp.max(y.reshape(32, 8, 128), axis=0))

    mxs[...] = lax.fori_loop(0, NR * NBLK, scale_step, jnp.zeros((8, 128), F32), unroll=4)
    mx_start, mx_wait, mx_drain = exchange(
        lambda to: mxs, lambda frm: mxr.at[frm], mx_s.at[0], mx_r.at[0], mxr.at[most], mxr.at[most]
    )
    each_peer(mx_start)
    mxr[f] = mxs[...]

    ga[1][3].wait_recv()
    rows_of(right)
    ga[1][2].wait_recv()
    rows_of(left)
    for i in (4, 5):
        ga[1][i].wait_recv()
    rows_of(far)

    mx_wait()
    mys[...] = jnp.max(mxr[...], axis=0)

    def my_copy(s):
        return remote(
            mys, myr.at[s - 1], my_s.at[s - 1], my_r.at[s - 1], (lax.rem(r + s, 4), f)
        )

    for s in (1, 2, 3):
        my_copy(s).start()

    ret_wait()

    def np0_step(t, carry):
        npf[t, :, :, cols(0)] = glob[t, :, :, cols(0)] - 0.7 * nrecv[t]
        return carry

    lax.fori_loop(0, NF, np0_step, 0, unroll=4)
    for s in (1, 2, 3):
        my_copy(s).wait_recv()
    top_out[...] = jnp.maximum(jnp.max(myr[...], axis=0), mys[...])
    for i in range(2, 6):
        gb[i].wait_recv()

    for p in (0, 1):
        for c in rs[p]:
            c.wait_send()
        for c in ga[p]:
            c.wait_send()
    for c in gb:
        c.wait_send()
    for d in (sc_drain, t_drain, gq0[2], gq1[2], ret_drain, mx_drain):
        d()
    for s in (1, 2, 3):
        my_copy(s).wait_send()


def writer(npf, mom, rot, top, np_out, nm_out, ns_out, sc_out, scaled, sem):
    first = pltpu.make_async_copy(npf, np_out, sem.at[0])
    second = pltpu.make_async_copy(mom, nm_out, sem.at[1])
    first.start()
    second.start()
    scale = jnp.max(top[...]) + 1e-06
    sc_out[0] = scale
    factor = 31.75 / jnp.broadcast_to(scale, (8, 128))
    wide = jnp.concatenate([factor] * (COLS // 128), axis=1)
    stores = []
    for i in range(NR):

        def step(t, carry, i=i):
            at = pl.ds(pl.multiple_of(t * COLS, 128), COLS)
            scaled[i, :, at] = rot[i, :, at] * wide
            return carry

        lax.fori_loop(0, NF, step, 0, unroll=4)
        stores.append(pltpu.make_async_copy(scaled.at[i], ns_out.at[i], sem.at[2 + i]))
        stores[-1].start()
    for c in [first, second] + stores:
        c.wait()


def body(global_params, local_params, flip_signs, momentum, stale_codes, stale_scale):
    shape = jax.ShapeDtypeStruct
    hbm = pl.BlockSpec(memory_space=pltpu.HBM)
    vmem = pl.BlockSpec(memory_space=pltpu.VMEM)
    smem = pl.BlockSpec(memory_space=pltpu.SMEM)
    dma = pltpu.SemaphoreType.DMA
    w0, w1 = PARTS[0][1], PARTS[1][1]
    col4, row4 = (NF, NR, 8, COLS), (NR, 8, FULL)

    def buf(*dims):
        return pltpu.VMEM(dims, F32)

    results = pl.pallas_call(
        kernel,
        out_shape=(shape(col4, F32), shape(row4, F32), shape(row4, F32), shape((8, 128), F32)),
        in_specs=[hbm, hbm, hbm, hbm, hbm, smem],
        out_specs=(vmem, vmem, vmem, vmem),
        scratch_shapes=[
            buf(*col4), buf(*col4), pltpu.VMEM((FULL // 128, 128), jnp.int32), buf(8, FULL), buf(*row4), buf(*row4),
            pltpu.VMEM((256, 128), BF16),
            buf(2, NF // 2, 8, w0), buf(2, NF // 2, 8, w1), buf(2, NF, 8, w0), buf(2, NF, 8, w1),
            buf(NF, 8, w0), buf(NF, 8, w1), buf(NR, NF, 8, w0), buf(NR, NF, 8, w1),
            buf(NF, 8, w1), buf(NF, 8, w1), buf(NF, NR, 8, w0), buf(NF, NR, 8, w0),
            buf(8, 128), buf(NF, 8, 128), buf(8, 128), buf(3, 8, 128),
            dma((11,)),
            dma((2, 6)), dma((2, 6)), dma((1,)), dma((1,)), dma((1,)), dma((1,)),
            dma((2,)), dma((2,)), dma((2, 6)), dma((2, 6)), dma((6,)), dma((6,)),
            dma((1,)), dma((1,)), dma((1,)), dma((1,)), dma((3,)), dma((3,)),
        ],
        compiler_params=pltpu.CompilerParams(
            collective_id=0, has_side_effects=True, vmem_limit_bytes=43 * 2**20
        ),
        name="outer_step",
    )(
        global_params.reshape(col4), local_params.reshape(col4), flip_signs.reshape(FULL // 128, 128),
        momentum.reshape(row4), stale_codes.reshape(row4), stale_scale,
    )
    new_params, new_momentum, new_stale, new_scale = pl.pallas_call(
        writer,
        out_shape=(shape(col4, F32), shape(row4, F32), shape(row4, F32), shape((1,), F32)),
        in_specs=[vmem] * 4,
        out_specs=(hbm, hbm, hbm, smem),
        scratch_shapes=[buf(*row4), dma((2 + NR,))],
        compiler_params=pltpu.CompilerParams(vmem_limit_bytes=16 * 2**20),
        name="write_results",
    )(*results)
    return (
        new_params.reshape(NF * NR * 8, COLS),
        new_momentum.reshape(NR * 8, FULL),
        new_stale.reshape(NR * 8, FULL),
        new_scale,
    )


def solution(mesh):
    placed = (
        P(None, "fsdp"),
        P("replica", None, "fsdp"),
        P(),
        P("fsdp", None),
        P("fsdp", None),
        P(),
    )
    return jax.shard_map(
        body,
        mesh=mesh,
        in_specs=placed,
        out_specs=(P(None, "fsdp"), P("fsdp", None), P("fsdp", None), P()),
        check_vma=False,
    )
```

```python
import jax
import jax.numpy as jnp
from jax import lax
from jax.experimental import pallas as pl
from jax.experimental.pallas import tpu as pltpu
from jax.sharding import PartitionSpec as P

MESH = pl.DeviceIdType.MESH
F32 = jnp.float32
BF16 = jnp.bfloat16
NF = 32
NR = 4
COLS = 896
FULL = NF * COLS
BLOCK = 4096
NBLK = FULL // BLOCK
PARTS = ((640, 256), (0, 640))
CUT = 1
HALF = (pl.ds(0, NF // 2), pl.ds(NF // 2, NF // 2))
ORDER = (4, 12, 1, 3, 5, 15, 7, 13, 8, 2, 9, 6, 11, 14, 10)
PACKED = [sum(v << (4 * i) for i, v in enumerate(ORDER[5 * k : 5 * k + 5])) for k in range(3)]


def fwht(value):
    width = value.shape[1]
    if width == 128:
        return [value]
    left, right = value[:, : width // 2], value[:, width // 2 :]
    return fwht(left + right) + fwht(left - right)


def kernel(
    glob_in, loc_in, flip_in, mom_in, stale_in, sscale_in,
    npf, mom, rot, top_out,
    glob, pg, signs, flips, stale, xrow, xpart, table,
    r1a, r1b, r2a, r2b, gqb, gra, grb, tsend, trecv, nsend, nrecv, mxs, mxr, mys, myr,
    ld_sem,
    rs_s, rs_r, sp_s, sp_r, sc_s, sc_r, t_s, t_r, gq_s, gq_r, ga_s, ga_r, gb_s, gb_r, ret_s, ret_r, mx_s, mx_r, my_s, my_r,
):
    r, f = lax.axis_index("replica"), lax.axis_index("fsdp")
    fx, fz, fc = f // 8, lax.rem(f // 2, 4), lax.rem(f, 2)
    right, left, far = lax.rem(r + 1, 4), lax.rem(r + 3, 4), lax.rem(r + 2, 4)
    to_right, to_left = (right, f), (left, f)

    def remote(src, dst, ss, rs, dev):
        return pltpu.make_async_remote_copy(
            src_ref=src, dst_ref=dst, send_sem=ss, recv_sem=rs, device_id=dev, device_id_type=MESH
        )

    def lanes(index, width=COLS, off=0):
        return pl.ds(pl.multiple_of(index * COLS + off, 128), width)

    def peers(s, dc):
        word = jnp.where(s < 5, PACKED[0], jnp.where(s < 10, PACKED[1], PACKED[2]))
        code = lax.rem(word >> (4 * lax.rem(s, 5)), 16)
        dx, dz = code // 4, lax.rem(code, 4)
        core = lax.rem(fc + dc, 2)
        to = lax.rem(fx + dx, 4) * 8 + lax.rem(fz + dz, 4) * 2 + core
        frm = lax.rem(fx + 4 - dx, 4) * 8 + lax.rem(fz + 4 - dz, 4) * 2 + core
        return to, frm

    other = f + 1 - 2 * fc

    def each_peer(fn, lo=0, hi=15, core=True):
        def step(s, carry):
            for dc in (0, 1):
                to, frm = peers(s, dc)
                fn(to, frm, 2 * s + dc)
            return carry

        lax.fori_loop(lo, hi, step, 0)
        if core:
            fn(other, other, 30)

    def exchange(src, dst, ss, rs, all_src, all_dst):
        def start(to, frm, i):
            remote(src(to), dst(f), ss, rs, (r, to)).start()

        def wait():
            remote(all_src, all_dst, ss, rs, (r, other)).wait_recv()

        def drain():
            remote(all_src, all_dst, ss, rs, (r, other)).wait_send()

        return start, wait, drain

    most = pl.ds(0, NF - 1)

    order = (far, right, left, r)
    loads = []
    for i, c in enumerate(order):
        a = pltpu.make_async_copy(loc_in.at[:, c], pg.at[:, c], ld_sem.at[2 * i])
        b = pltpu.make_async_copy(glob_in.at[:, c], glob.at[:, c], ld_sem.at[2 * i + 1])
        a.start()
        b.start()
        loads.append((a, b))
    ld_stale = pltpu.make_async_copy(stale_in, stale, ld_sem.at[8])
    ld_mom = pltpu.make_async_copy(mom_in, mom, ld_sem.at[9])
    ld_signs = pltpu.make_async_copy(flip_in, signs, ld_sem.at[10])
    ld_signs.start()
    ld_stale.start()
    ld_mom.start()

    barrier = pltpu.get_barrier_semaphore()

    def greet(s, carry):
        pl.semaphore_signal(
            barrier, inc=1, device_id=(r, lax.rem(f + s, NF)), device_id_type=MESH
        )
        return carry

    lax.fori_loop(1, NF, greet, 0)
    for s in (1, 2, 3):
        pl.semaphore_signal(barrier, inc=1, device_id=(lax.rem(r + s, 4), f), device_id_type=MESH)

    def difference(i):
        c = order[i]
        for load in loads[i]:
            load.wait()

        def diff(t, carry):
            rows = pl.ds(4 * t, 4)
            pg[rows, c] = glob[rows, c] - pg[rows, c]
            return carry

        lax.fori_loop(0, NF // 4, diff, 0, unroll=2)

    difference(0)
    pl.semaphore_wait(barrier, NF - 1 + NR - 1)

    r1 = (r1a, r1b)
    r2 = (r2a, r2b)
    gr = (gra, grb)

    def cols(p):
        return pl.ds(PARTS[p][0], PARTS[p][1])

    def term(p, half, c):
        return xpart.at[c, half] if p == 0 else pg.at[half, c, :, cols(1)]

    def rs_copies(p):
        lo, hi = HALF
        return (
            remote(term(p, lo, far), r1[p].at[0], rs_s.at[p, 0], rs_r.at[p, 0], to_right),
            remote(term(p, hi, far), r1[p].at[1], rs_s.at[p, 1], rs_r.at[p, 1], to_left),
            remote(term(p, hi, right), r2[p].at[0, hi], rs_s.at[p, 2], rs_r.at[p, 2], to_right),
            remote(term(p, lo, left), r2[p].at[1, lo], rs_s.at[p, 3], rs_r.at[p, 3], to_left),
            remote(r1[p].at[0], r2[p].at[0, lo], rs_s.at[p, 4], rs_r.at[p, 4], to_right),
            remote(r1[p].at[1], r2[p].at[1, hi], rs_s.at[p, 5], rs_r.at[p, 5], to_left),
        )

    rs = (rs_copies(0), rs_copies(1))

    def rs_second(p):
        for side, c, base in ((0, right, 0), (1, left, NF // 2)):
            rs[p][side].wait_recv()

            def add(t, carry, side=side, c=c, base=base):
                rows = pl.ds(4 * t, 4)
                r1[p][side, rows] = r1[p][side, rows] + term(p, pl.ds(base + 4 * t, 4), c)[...]
                return carry

            lax.fori_loop(0, NF // 8, add, 0, unroll=2)
            rs[p][4 + side].start()

    def rs_last(p):
        for i in range(2, 6):
            rs[p][i].wait_recv()

        def add(t, carry):
            rows = pl.ds(4 * t, 4)
            total = term(p, rows, r)[...] + (r2[p][0, rows] + r2[p][1, rows])
            if p == 0:
                gra[r, rows] = total
            else:
                gqb[rows] = total
            return carry

        lax.fori_loop(0, NF // 4, add, 0, unroll=2)

    for i in (0, 1):
        rs[1][i].start()
    difference(1)
    difference(2)
    for i in (2, 3):
        rs[1][i].start()
    difference(3)

    off1, wid1 = PARTS[1]
    off0, wid0 = PARTS[0]
    sp_start, sp_wait, sp_drain = exchange(
        lambda to: pg.at[to, :, :, cols(0)], lambda frm: xpart.at[:, frm], sp_s.at[0], sp_r.at[0],
        pg.at[most, :, :, cols(0)], xpart.at[:, most],
    )
    sc_start, sc_wait, sc_drain = exchange(
        lambda to: pg.at[to, :, :, cols(1)], lambda frm: xrow.at[:, :, lanes(frm, wid1, off1)],
        sc_s.at[0], sc_r.at[0], pg.at[most, :, :, cols(1)], xrow.at[:, :, pl.ds(0, (NF - 1) * wid1)],
    )
    each_peer(sp_start)
    for i in range(NR):
        xpart[i, f] = pg[f, i, :, cols(0)]
        xrow[i, :, lanes(f, wid1, off1)] = pg[f, i, :, cols(1)]

    ld_signs.wait()

    def flip_step(t, carry):
        rows = (2 * signs[pl.ds(8 * t, 8), :] - 1).astype(F32)
        flips[:, pl.ds(pl.multiple_of(t * 1024, 1024), 1024)] = jnp.concatenate(
            [jnp.broadcast_to(rows[i : i + 1], (8, 128)) for i in range(8)], axis=1
        )
        return carry

    lax.fori_loop(0, FULL // 1024, flip_step, 0, unroll=2)
    bits = lax.broadcasted_iota(jnp.int32, (256, 128), 0) & lax.broadcasted_iota(jnp.int32, (256, 128), 1)
    parity = jnp.zeros((256, 128), jnp.int32)
    for b in range(7):
        parity = parity ^ (bits >> b)
    table[...] = jnp.where((parity & 1) == 0, 1.0 / 64.0, -1.0 / 64.0).astype(F32).astype(BF16)

    def hadamard(value):
        x = jnp.concatenate(fwht(value), axis=0)
        high = x.astype(BF16)
        low = (x - high.astype(F32)).astype(BF16)
        return jnp.dot(
            jnp.concatenate([high, low], axis=1), table[...], preferred_element_type=F32
        )

    def to_rows(value):
        return jnp.concatenate([value[8 * a : 8 * a + 8] for a in range(32)], axis=1)

    def blk(k):
        return pl.ds(pl.multiple_of(k * BLOCK, BLOCK), BLOCK)

    coef = 0.5 * (sscale_in[0] / 127.0)
    ld_stale.wait()

    def stale_step(t, carry):
        i, k = t // NBLK, lax.rem(t, NBLK)
        stale[i, :, blk(k)] = to_rows(hadamard(stale[i, :, blk(k)])) * (flips[:, blk(k)] * coef)
        return carry

    lax.fori_loop(0, NR * NBLK, stale_step, 0, unroll=4)
    ld_mom.wait()

    def t_step(g, carry):
        tsend[g] = 1.9 * stale[r, :, lanes(g, wid1, off1)] + 0.81 * mom[r, :, lanes(g, wid1, off1)]
        return carry

    lax.fori_loop(0, NF, t_step, 0, unroll=4)
    t_start, t_wait, t_drain = exchange(
        lambda to: tsend.at[to], lambda frm: trecv.at[frm], t_s.at[0], t_r.at[0],
        tsend.at[most], trecv.at[most],
    )
    each_peer(t_start)
    trecv[f] = tsend[f]

    each_peer(sc_start, 0, CUT, True)

    gq_start, gq_wait, gq_drain = exchange(
        lambda to: gqb.at[to], lambda frm: grb.at[r, frm], gq_s.at[0], gq_r.at[0],
        gqb.at[most], grb.at[r, most],
    )

    def gather(ref, ss, sr):
        return (
            remote(ref(r, 0), ref(r, 0), ss.at[0], sr.at[0], to_right),
            remote(ref(r, 1), ref(r, 1), ss.at[1], sr.at[1], to_left),
            remote(ref(r, 1), ref(r, 1), ss.at[2], sr.at[2], to_right),
            remote(ref(r, 0), ref(r, 0), ss.at[3], sr.at[3], to_left),
            remote(ref(left, 0), ref(left, 0), ss.at[4], sr.at[4], to_right),
            remote(ref(right, 1), ref(right, 1), ss.at[5], sr.at[5], to_left),
        )

    ga = [
        gather(lambda c, h, p=p: gr[p].at[c, HALF[h]], ga_s.at[p], ga_r.at[p]) for p in (0, 1)
    ]
    gb = gather(lambda c, h: npf.at[HALF[h], c, :, cols(1)], gb_s, gb_r)

    def gather_start(g):
        for i in range(4):
            g[i].start()

    def gather_forward(g):
        for i in range(2):
            g[i].wait_recv()
            g[4 + i].start()

    def rows_of(i):
        def mom_step(g, carry):
            for p, (off, wid) in enumerate(PARTS):
                at = lanes(g, wid, off)
                v = gr[p][i, g]
                mom[i, :, at] = 0.9 * mom[i, :, at] + (0.125 * v + stale[i, :, at])
                rot[i, :, at] = v * flips[:, at]
            return carry

        lax.fori_loop(0, NF, mom_step, 0, unroll=4)

        def rot_step(k, carry):
            rot[i, :, blk(k)] = to_rows(hadamard(rot[i, :, blk(k)]))
            return carry

        lax.fori_loop(0, NBLK, rot_step, 0, unroll=NBLK)

    rs_second(1)
    sp_wait()
    for i in range(4):
        rs[0][i].start()

    def part_step(t, carry):
        i, g = t // NF, lax.rem(t, NF)
        xrow[i, :, lanes(g, wid0, off0)] = xpart[i, g]
        return carry

    lax.fori_loop(0, NR * NF, part_step, 0, unroll=4)

    rs_last(1)
    each_peer(gq_start)
    each_peer(sc_start, CUT, 15, False)
    grb[r, f] = gqb[f]
    t_wait()

    def np_step(t, carry):
        rows = pl.ds(4 * t, 4)
        npf[rows, r, :, cols(1)] = glob[rows, r, :, cols(1)] - 0.7 * (trecv[rows] + 0.2375 * gqb[rows])
        return carry

    lax.fori_loop(0, NF // 4, np_step, 0, unroll=2)
    rs_second(0)
    for i in (0, 1):
        gb[i].start()
    rs_last(0)
    gather_start(ga[0])
    gather_forward(ga[0])
    for i in (2, 3):
        gb[i].start()
    gq_wait()
    gather_start(ga[1])

    for i in range(2, 6):
        ga[0][i].wait_recv()

    def n_step(t, carry):
        i, g = t // NF, lax.rem(t, NF)
        nsend[g, i] = (
            1.9 * (0.125 * gra[i, g] + stale[i, :, lanes(g, wid0, off0)])
            + 0.81 * mom[i, :, lanes(g, wid0, off0)]
        )
        return carry

    lax.fori_loop(0, NR * NF, n_step, 0, unroll=4)
    ret_start, ret_wait, ret_drain = exchange(
        lambda to: nsend.at[to], lambda frm: nrecv.at[frm], ret_s.at[0], ret_r.at[0],
        nsend.at[most], nrecv.at[most],
    )
    each_peer(ret_start)
    nrecv[f] = nsend[f]

    rows_of(r)
    gather_forward(ga[1])
    gather_forward(gb)

    sc_wait()

    def scale_step(t, top):
        i, k = t // NBLK, lax.rem(t, NBLK)
        y = jnp.abs(hadamard(xrow[i, :, blk(k)] * flips[:, blk(k)]))
        return jnp.maximum(top, jnp.max(y.reshape(32, 8, 128), axis=0))

    mxs[...] = lax.fori_loop(0, NR * NBLK, scale_step, jnp.zeros((8, 128), F32), unroll=4)
    mx_start, mx_wait, mx_drain = exchange(
        lambda to: mxs, lambda frm: mxr.at[frm], mx_s.at[0], mx_r.at[0], mxr.at[most], mxr.at[most]
    )
    each_peer(mx_start)
    mxr[f] = mxs[...]

    ga[1][3].wait_recv()
    rows_of(right)
    ga[1][2].wait_recv()
    rows_of(left)
    for i in (4, 5):
        ga[1][i].wait_recv()
    rows_of(far)

    mx_wait()
    mys[...] = jnp.max(mxr[...], axis=0)

    def my_copy(s):
        return remote(
            mys, myr.at[s - 1], my_s.at[s - 1], my_r.at[s - 1], (lax.rem(r + s, 4), f)
        )

    for s in (1, 2, 3):
        my_copy(s).start()

    ret_wait()

    def np0_step(t, carry):
        npf[t, :, :, cols(0)] = glob[t, :, :, cols(0)] - 0.7 * nrecv[t]
        return carry

    lax.fori_loop(0, NF, np0_step, 0, unroll=4)
    for s in (1, 2, 3):
        my_copy(s).wait_recv()
    top_out[...] = jnp.maximum(jnp.max(myr[...], axis=0), mys[...])
    for i in range(2, 6):
        gb[i].wait_recv()

    for p in (0, 1):
        for c in rs[p]:
            c.wait_send()
        for c in ga[p]:
            c.wait_send()
    for c in gb:
        c.wait_send()
    for d in (sp_drain, sc_drain, t_drain, gq_drain, ret_drain, mx_drain):
        d()
    for s in (1, 2, 3):
        my_copy(s).wait_send()


def writer(npf, mom, rot, top, np_out, nm_out, ns_out, sc_out, scaled, sem):
    first = pltpu.make_async_copy(npf, np_out, sem.at[0])
    second = pltpu.make_async_copy(mom, nm_out, sem.at[1])
    first.start()
    second.start()
    scale = jnp.max(top[...]) + 1e-06
    sc_out[0] = scale
    factor = 31.75 / jnp.broadcast_to(scale, (8, 128))
    wide = jnp.concatenate([factor] * (COLS // 128), axis=1)
    stores = []
    for i in range(NR):

        def step(t, carry, i=i):
            at = pl.ds(pl.multiple_of(t * COLS, 128), COLS)
            scaled[i, :, at] = rot[i, :, at] * wide
            return carry

        lax.fori_loop(0, NF, step, 0, unroll=4)
        stores.append(pltpu.make_async_copy(scaled.at[i], ns_out.at[i], sem.at[2 + i]))
        stores[-1].start()
    for c in [first, second] + stores:
        c.wait()


def body(global_params, local_params, flip_signs, momentum, stale_codes, stale_scale):
    shape = jax.ShapeDtypeStruct
    hbm = pl.BlockSpec(memory_space=pltpu.HBM)
    vmem = pl.BlockSpec(memory_space=pltpu.VMEM)
    smem = pl.BlockSpec(memory_space=pltpu.SMEM)
    dma = pltpu.SemaphoreType.DMA
    w0, w1 = PARTS[0][1], PARTS[1][1]
    col4, row4 = (NF, NR, 8, COLS), (NR, 8, FULL)

    def buf(*dims):
        return pltpu.VMEM(dims, F32)

    results = pl.pallas_call(
        kernel,
        out_shape=(shape(col4, F32), shape(row4, F32), shape(row4, F32), shape((8, 128), F32)),
        in_specs=[hbm, hbm, hbm, hbm, hbm, smem],
        out_specs=(vmem, vmem, vmem, vmem),
        scratch_shapes=[
            buf(*col4), buf(*col4), pltpu.VMEM((FULL // 128, 128), jnp.int32), buf(8, FULL), buf(*row4), buf(*row4),
            buf(NR, NF, 8, w0), pltpu.VMEM((256, 128), BF16),
            buf(2, NF // 2, 8, w0), buf(2, NF // 2, 8, w1), buf(2, NF, 8, w0), buf(2, NF, 8, w1),
            buf(NF, 8, w1), buf(NR, NF, 8, w0), buf(NR, NF, 8, w1),
            buf(NF, 8, w1), buf(NF, 8, w1), buf(NF, NR, 8, w0), buf(NF, NR, 8, w0),
            buf(8, 128), buf(NF, 8, 128), buf(8, 128), buf(3, 8, 128),
            dma((11,)),
            dma((2, 6)), dma((2, 6)), dma((1,)), dma((1,)), dma((1,)), dma((1,)), dma((1,)), dma((1,)),
            dma((1,)), dma((1,)), dma((2, 6)), dma((2, 6)), dma((6,)), dma((6,)),
            dma((1,)), dma((1,)), dma((1,)), dma((1,)), dma((3,)), dma((3,)),
        ],
        compiler_params=pltpu.CompilerParams(
            collective_id=0, has_side_effects=True, vmem_limit_bytes=43 * 2**20
        ),
        name="outer_step",
    )(
        global_params.reshape(col4), local_params.reshape(col4), flip_signs.reshape(FULL // 128, 128),
        momentum.reshape(row4), stale_codes.reshape(row4), stale_scale,
    )
    new_params, new_momentum, new_stale, new_scale = pl.pallas_call(
        writer,
        out_shape=(shape(col4, F32), shape(row4, F32), shape(row4, F32), shape((1,), F32)),
        in_specs=[vmem] * 4,
        out_specs=(hbm, hbm, hbm, smem),
        scratch_shapes=[buf(*row4), dma((2 + NR,))],
        compiler_params=pltpu.CompilerParams(vmem_limit_bytes=16 * 2**20),
        name="write_results",
    )(*results)
    return (
        new_params.reshape(NF * NR * 8, COLS),
        new_momentum.reshape(NR * 8, FULL),
        new_stale.reshape(NR * 8, FULL),
        new_scale,
    )


def solution(mesh):
    placed = (
        P(None, "fsdp"),
        P("replica", None, "fsdp"),
        P(),
        P("fsdp", None),
        P("fsdp", None),
        P(),
    )
    return jax.shard_map(
        body,
        mesh=mesh,
        in_specs=placed,
        out_specs=(P(None, "fsdp"), P("fsdp", None), P("fsdp", None), P()),
        check_vma=False,
    )
```

```python
import jax
import jax.numpy as jnp
from jax import lax
from jax.experimental import pallas as pl
from jax.experimental.pallas import tpu as pltpu
from jax.sharding import PartitionSpec as P

MESH = pl.DeviceIdType.MESH
F32 = jnp.float32
BF16 = jnp.bfloat16
NF = 32
NR = 4
COLS = 896
FULL = NF * COLS
BLOCK = 4096
NBLK = FULL // BLOCK
PARTS = ((512, 384), (0, 512))
CUT = 1
HALF = (pl.ds(0, NF // 2), pl.ds(NF // 2, NF // 2))
ORDER = (4, 12, 1, 3, 5, 15, 7, 13, 8, 2, 9, 6, 11, 14, 10)
PACKED = [sum(v << (4 * i) for i, v in enumerate(ORDER[5 * k : 5 * k + 5])) for k in range(3)]


def fwht(value):
    width = value.shape[1]
    if width == 128:
        return [value]
    left, right = value[:, : width // 2], value[:, width // 2 :]
    return fwht(left + right) + fwht(left - right)


def kernel(
    glob_in, loc_in, flip_in, mom_in, stale_in, sscale_in,
    npf, mom, rot, top_out,
    glob, pg, signs, flips, stale, xrow, xpart, table,
    r1a, r1b, r2a, r2b, gqb, gra, grb, tsend, trecv, nsend, nrecv, mxs, mxr, mys, myr,
    ld_sem,
    rs_s, rs_r, sp_s, sp_r, sc_s, sc_r, t_s, t_r, gq_s, gq_r, ga_s, ga_r, gb_s, gb_r, ret_s, ret_r, mx_s, mx_r, my_s, my_r,
):
    r, f = lax.axis_index("replica"), lax.axis_index("fsdp")
    fx, fz, fc = f // 8, lax.rem(f // 2, 4), lax.rem(f, 2)
    right, left, far = lax.rem(r + 1, 4), lax.rem(r + 3, 4), lax.rem(r + 2, 4)
    to_right, to_left = (right, f), (left, f)

    def remote(src, dst, ss, rs, dev):
        return pltpu.make_async_remote_copy(
            src_ref=src, dst_ref=dst, send_sem=ss, recv_sem=rs, device_id=dev, device_id_type=MESH
        )

    def lanes(index, width=COLS, off=0):
        return pl.ds(pl.multiple_of(index * COLS + off, 128), width)

    def peers(s, dc):
        word = jnp.where(s < 5, PACKED[0], jnp.where(s < 10, PACKED[1], PACKED[2]))
        code = lax.rem(word >> (4 * lax.rem(s, 5)), 16)
        dx, dz = code // 4, lax.rem(code, 4)
        core = lax.rem(fc + dc, 2)
        to = lax.rem(fx + dx, 4) * 8 + lax.rem(fz + dz, 4) * 2 + core
        frm = lax.rem(fx + 4 - dx, 4) * 8 + lax.rem(fz + 4 - dz, 4) * 2 + core
        return to, frm

    other = f + 1 - 2 * fc

    def each_peer(fn, lo=0, hi=15, core=True):
        def step(s, carry):
            for dc in (0, 1):
                to, frm = peers(s, dc)
                fn(to, frm, 2 * s + dc)
            return carry

        lax.fori_loop(lo, hi, step, 0)
        if core:
            fn(other, other, 30)

    def exchange(src, dst, ss, rs, all_src, all_dst):
        def start(to, frm, i):
            remote(src(to), dst(f), ss, rs, (r, to)).start()

        def wait():
            remote(all_src, all_dst, ss, rs, (r, other)).wait_recv()

        def drain():
            remote(all_src, all_dst, ss, rs, (r, other)).wait_send()

        return start, wait, drain

    most = pl.ds(0, NF - 1)

    order = ((far, 2), (left, 3), (right, 1), (r, 0))
    loads = []
    for i, (c, j) in enumerate(order):
        a = pltpu.make_async_copy(loc_in.at[:, c], pg.at[:, j], ld_sem.at[2 * i])
        b = pltpu.make_async_copy(glob_in.at[:, c], glob.at[:, c], ld_sem.at[2 * i + 1])
        loads.append((a, b))
    ld_stale = pltpu.make_async_copy(stale_in, stale, ld_sem.at[8])
    ld_mom = pltpu.make_async_copy(mom_in, mom, ld_sem.at[9])
    ld_signs = pltpu.make_async_copy(flip_in, signs, ld_sem.at[10])
    for load in loads[0]:
        load.start()

    barrier = pltpu.get_barrier_semaphore()

    for s in (1, 2, 3):
        pl.semaphore_signal(barrier, inc=1, device_id=(lax.rem(r + s, 4), f), device_id_type=MESH)

    def greet(s, carry):
        pl.semaphore_signal(
            barrier, inc=1, device_id=(r, lax.rem(f + s, NF)), device_id_type=MESH
        )
        return carry

    lax.fori_loop(1, NF, greet, 0)

    def difference(i):
        c, j = order[i]
        for load in loads[i]:
            load.wait()

        def diff(t, carry):
            rows = pl.ds(4 * t, 4)
            pg[rows, j] = glob[rows, c] - pg[rows, j]
            return carry

        lax.fori_loop(0, NF // 4, diff, 0, unroll=2)

    for i in (1, 2, 3):
        for load in loads[i]:
            load.start()
    difference(0)
    pl.semaphore_wait(barrier, NF - 1 + NR - 1)

    r1 = (r1a, r1b)
    r2 = (r2a, r2b)
    gr = (gra, grb)

    def cols(p):
        return pl.ds(PARTS[p][0], PARTS[p][1])

    def term(p, half, j):
        return xpart.at[j, half] if p == 0 else pg.at[half, j, :, cols(1)]

    def rs_copies(p):
        lo, hi = HALF
        return (
            remote(term(p, lo, 2), r1[p].at[0], rs_s.at[p, 0], rs_r.at[p, 0], to_right),
            remote(term(p, hi, 2), r1[p].at[1], rs_s.at[p, 1], rs_r.at[p, 1], to_left),
            remote(term(p, hi, 1), r2[p].at[0, hi], rs_s.at[p, 2], rs_r.at[p, 2], to_right),
            remote(term(p, lo, 3), r2[p].at[1, lo], rs_s.at[p, 3], rs_r.at[p, 3], to_left),
            remote(r1[p].at[0], r2[p].at[0, lo], rs_s.at[p, 4], rs_r.at[p, 4], to_right),
            remote(r1[p].at[1], r2[p].at[1, hi], rs_s.at[p, 5], rs_r.at[p, 5], to_left),
        )

    rs = (rs_copies(0), rs_copies(1))

    def rs_second(p):
        for side, j, base in ((0, 1, 0), (1, 3, NF // 2)):
            rs[p][side].wait_recv()

            def add(t, carry, side=side, j=j, base=base):
                rows = pl.ds(4 * t, 4)
                r1[p][side, rows] = r1[p][side, rows] + term(p, pl.ds(base + 4 * t, 4), j)[...]
                return carry

            lax.fori_loop(0, NF // 8, add, 0, unroll=2)
            rs[p][4 + side].start()

    def rs_last(p):
        for i in range(2, 6):
            rs[p][i].wait_recv()

        def add(t, carry):
            rows = pl.ds(4 * t, 4)
            total = term(p, rows, 0)[...] + (r2[p][0, rows] + r2[p][1, rows])
            if p == 0:
                gra[r, rows] = total
            else:
                gqb[rows] = total
            return carry

        lax.fori_loop(0, NF // 4, add, 0, unroll=2)

    for i in (0, 1):
        rs[1][i].start()
    ld_signs.start()
    ld_stale.start()
    ld_mom.start()
    difference(1)
    difference(2)
    for i in (3, 2):
        rs[1][i].start()
    difference(3)

    off1, wid1 = PARTS[1]
    off0, wid0 = PARTS[0]
    def sp_exchange(k):
        pair = pl.ds(2 * k, 2)
        return exchange(
            lambda to: pg.at[to, pair, :, cols(0)], lambda frm: xpart.at[pair, frm],
            sp_s.at[k], sp_r.at[k], pg.at[most, pair, :, cols(0)], xpart.at[pair, most],
        )

    sp = (sp_exchange(0), sp_exchange(1))
    sc_start, sc_wait, sc_drain = exchange(
        lambda to: pg.at[to, :, :, cols(1)], lambda frm: xrow.at[:, :, lanes(frm, wid1, off1)],
        sc_s.at[0], sc_r.at[0], pg.at[most, :, :, cols(1)], xrow.at[:, :, pl.ds(0, (NF - 1) * wid1)],
    )
    each_peer(sp[1][0])
    each_peer(sp[0][0])
    for i in range(NR):
        xpart[i, f] = pg[f, i, :, cols(0)]
        xrow[i, :, lanes(f, wid1, off1)] = pg[f, i, :, cols(1)]

    ld_signs.wait()

    def flip_step(t, carry):
        rows = (2 * signs[pl.ds(8 * t, 8), :] - 1).astype(F32)
        flips[:, pl.ds(pl.multiple_of(t * 1024, 1024), 1024)] = jnp.concatenate(
            [jnp.broadcast_to(rows[i : i + 1], (8, 128)) for i in range(8)], axis=1
        )
        return carry

    lax.fori_loop(0, FULL // 1024, flip_step, 0, unroll=2)
    bits = lax.broadcasted_iota(jnp.int32, (256, 128), 0) & lax.broadcasted_iota(jnp.int32, (256, 128), 1)
    parity = jnp.zeros((256, 128), jnp.int32)
    for b in range(7):
        parity = parity ^ (bits >> b)
    table[...] = jnp.where((parity & 1) == 0, 1.0 / 64.0, -1.0 / 64.0).astype(F32).astype(BF16)

    def hadamard(value):
        x = jnp.concatenate(fwht(value), axis=0)
        high = x.astype(BF16)
        low = (x - high.astype(F32)).astype(BF16)
        return jnp.dot(
            jnp.concatenate([high, low], axis=1), table[...], preferred_element_type=F32
        )

    def to_rows(value):
        return jnp.concatenate([value[8 * a : 8 * a + 8] for a in range(32)], axis=1)

    def blk(k):
        return pl.ds(pl.multiple_of(k * BLOCK, BLOCK), BLOCK)

    coef = 0.5 * (sscale_in[0] / 127.0)
    ld_stale.wait()

    def stale_step(t, carry):
        i, k = t // NBLK, lax.rem(t, NBLK)
        stale[i, :, blk(k)] = to_rows(hadamard(stale[i, :, blk(k)])) * (flips[:, blk(k)] * coef)
        return carry

    lax.fori_loop(0, NR * NBLK, stale_step, 0, unroll=4)
    ld_mom.wait()

    def t_step(g, carry):
        tsend[g] = 1.9 * stale[r, :, lanes(g, wid1, off1)] + 0.81 * mom[r, :, lanes(g, wid1, off1)]
        return carry

    lax.fori_loop(0, NF, t_step, 0, unroll=4)
    t_start, t_wait, t_drain = exchange(
        lambda to: tsend.at[to], lambda frm: trecv.at[frm], t_s.at[0], t_r.at[0],
        tsend.at[most], trecv.at[most],
    )
    each_peer(t_start)
    trecv[f] = tsend[f]

    each_peer(sc_start, 0, CUT, True)

    gq_start, gq_wait, gq_drain = exchange(
        lambda to: gqb.at[to], lambda frm: grb.at[r, frm], gq_s.at[0], gq_r.at[0],
        gqb.at[most], grb.at[r, most],
    )

    def gather(ref, ss, sr):
        return (
            remote(ref(r, 0), ref(r, 0), ss.at[0], sr.at[0], to_right),
            remote(ref(r, 1), ref(r, 1), ss.at[1], sr.at[1], to_left),
            remote(ref(r, 1), ref(r, 1), ss.at[2], sr.at[2], to_right),
            remote(ref(r, 0), ref(r, 0), ss.at[3], sr.at[3], to_left),
            remote(ref(left, 0), ref(left, 0), ss.at[4], sr.at[4], to_right),
            remote(ref(right, 1), ref(right, 1), ss.at[5], sr.at[5], to_left),
        )

    ga = [
        gather(lambda c, h, p=p: gr[p].at[c, HALF[h]], ga_s.at[p], ga_r.at[p]) for p in (0, 1)
    ]
    gb = gather(lambda c, h: npf.at[HALF[h], c, :, cols(1)], gb_s, gb_r)

    def gather_start(g):
        for i in range(4):
            g[i].start()

    def gather_forward(g):
        for i in range(2):
            g[i].wait_recv()
            g[4 + i].start()

    def rows_of(i):
        def mom_step(g, carry):
            for p, (off, wid) in enumerate(PARTS):
                at = lanes(g, wid, off)
                v = gr[p][i, g]
                mom[i, :, at] = 0.9 * mom[i, :, at] + (0.125 * v + stale[i, :, at])
                rot[i, :, at] = v * flips[:, at]
            return carry

        lax.fori_loop(0, NF, mom_step, 0, unroll=4)

        def rot_step(k, carry):
            rot[i, :, blk(k)] = to_rows(hadamard(rot[i, :, blk(k)]))
            return carry

        lax.fori_loop(0, NBLK, rot_step, 0, unroll=NBLK)

    rs_second(1)
    sp[1][1]()
    for i in (0, 1, 3):
        rs[0][i].start()
    sp[0][1]()
    rs[0][2].start()

    def part_step(t, carry):
        i, g = t // NF, lax.rem(t, NF)
        xrow[i, :, lanes(g, wid0, off0)] = xpart[i, g]
        return carry

    lax.fori_loop(0, NR * NF, part_step, 0, unroll=4)

    rs_last(1)
    each_peer(gq_start)
    each_peer(sc_start, CUT, 15, False)
    grb[r, f] = gqb[f]
    t_wait()

    def np_step(t, carry):
        rows = pl.ds(4 * t, 4)
        npf[rows, r, :, cols(1)] = glob[rows, r, :, cols(1)] - 0.7 * (trecv[rows] + 0.2375 * gqb[rows])
        return carry

    lax.fori_loop(0, NF // 4, np_step, 0, unroll=2)
    rs_second(0)
    for i in (0, 1):
        gb[i].start()
    rs_last(0)
    gather_start(ga[0])
    gather_forward(ga[0])
    for i in (2, 3):
        gb[i].start()
    gq_wait()
    gather_start(ga[1])

    for i in range(2, 6):
        ga[0][i].wait_recv()

    def n_step(t, carry):
        i, g = t // NF, lax.rem(t, NF)
        nsend[g, i] = (
            1.9 * (0.125 * gra[i, g] + stale[i, :, lanes(g, wid0, off0)])
            + 0.81 * mom[i, :, lanes(g, wid0, off0)]
        )
        return carry

    lax.fori_loop(0, NR * NF, n_step, 0, unroll=4)
    ret_start, ret_wait, ret_drain = exchange(
        lambda to: nsend.at[to], lambda frm: nrecv.at[frm], ret_s.at[0], ret_r.at[0],
        nsend.at[most], nrecv.at[most],
    )
    each_peer(ret_start, 0, 6, False)
    nrecv[f] = nsend[f]

    rows_of(r)
    sc_wait()

    def scale_step(t, top):
        i, k = t // NBLK, lax.rem(t, NBLK)
        y = jnp.abs(hadamard(xrow[i, :, blk(k)] * flips[:, blk(k)]))
        return jnp.maximum(top, jnp.max(y.reshape(32, 8, 128), axis=0))

    mxs[...] = lax.fori_loop(0, NR * NBLK, scale_step, jnp.zeros((8, 128), F32), unroll=4)
    mx_start, mx_wait, mx_drain = exchange(
        lambda to: mxs, lambda frm: mxr.at[frm], mx_s.at[0], mx_r.at[0], mxr.at[most], mxr.at[most]
    )
    each_peer(mx_start)
    each_peer(ret_start, 6, 15, True)
    mxr[f] = mxs[...]

    gather_forward(ga[1])
    gather_forward(gb)

    ga[1][3].wait_recv()
    rows_of(right)
    ga[1][2].wait_recv()
    rows_of(left)
    for i in (4, 5):
        ga[1][i].wait_recv()
    rows_of(far)

    mx_wait()
    mys[...] = jnp.max(mxr[...], axis=0)

    def my_copy(s):
        return remote(
            mys, myr.at[s - 1], my_s.at[s - 1], my_r.at[s - 1], (lax.rem(r + s, 4), f)
        )

    for s in (1, 2, 3):
        my_copy(s).start()

    ret_wait()

    def np0_step(t, carry):
        npf[t, :, :, cols(0)] = glob[t, :, :, cols(0)] - 0.7 * nrecv[t]
        return carry

    lax.fori_loop(0, NF, np0_step, 0, unroll=4)
    for s in (1, 2, 3):
        my_copy(s).wait_recv()
    top_out[...] = jnp.maximum(jnp.max(myr[...], axis=0), mys[...])
    for i in range(2, 6):
        gb[i].wait_recv()

    for p in (0, 1):
        for c in rs[p]:
            c.wait_send()
        for c in ga[p]:
            c.wait_send()
    for c in gb:
        c.wait_send()
    for d in (sp[0][2], sp[1][2], sc_drain, t_drain, gq_drain, ret_drain, mx_drain):
        d()
    for s in (1, 2, 3):
        my_copy(s).wait_send()


def writer(npf, mom, rot, top, np_out, nm_out, ns_out, sc_out, scaled, sem):
    stores = []
    for i in range(NR):
        rows = pl.ds(8 * i, 8)
        stores.append(pltpu.make_async_copy(npf.at[rows], np_out.at[rows], sem.at[i]))
        stores.append(pltpu.make_async_copy(mom.at[i], nm_out.at[i], sem.at[4 + i]))
    for c in stores:
        c.start()
    scale = jnp.max(top[...]) + 1e-06
    sc_out[0] = scale
    factor = 31.75 / jnp.broadcast_to(scale, (8, 128))
    wide = jnp.concatenate([factor] * (COLS // 128), axis=1)
    for i in range(NR):

        def step(t, carry, i=i):
            at = pl.ds(pl.multiple_of(t * COLS, 128), COLS)
            scaled[i, :, at] = rot[i, :, at] * wide
            return carry

        lax.fori_loop(0, NF, step, 0, unroll=4)
        stores.append(pltpu.make_async_copy(scaled.at[i], ns_out.at[i], sem.at[8 + i]))
        stores[-1].start()
    for c in stores:
        c.wait()


def body(global_params, local_params, flip_signs, momentum, stale_codes, stale_scale):
    shape = jax.ShapeDtypeStruct
    hbm = pl.BlockSpec(memory_space=pltpu.HBM)
    vmem = pl.BlockSpec(memory_space=pltpu.VMEM)
    smem = pl.BlockSpec(memory_space=pltpu.SMEM)
    dma = pltpu.SemaphoreType.DMA
    w0, w1 = PARTS[0][1], PARTS[1][1]
    col4, row4 = (NF, NR, 8, COLS), (NR, 8, FULL)

    def buf(*dims):
        return pltpu.VMEM(dims, F32)

    results = pl.pallas_call(
        kernel,
        out_shape=(shape(col4, F32), shape(row4, F32), shape(row4, F32), shape((8, 128), F32)),
        in_specs=[hbm, hbm, hbm, hbm, hbm, smem],
        out_specs=(vmem, vmem, vmem, vmem),
        scratch_shapes=[
            buf(*col4), buf(*col4), pltpu.VMEM((FULL // 128, 128), jnp.int32), buf(8, FULL), buf(*row4), buf(*row4),
            buf(NR, NF, 8, w0), pltpu.VMEM((256, 128), BF16),
            buf(2, NF // 2, 8, w0), buf(2, NF // 2, 8, w1), buf(2, NF, 8, w0), buf(2, NF, 8, w1),
            buf(NF, 8, w1), buf(NR, NF, 8, w0), buf(NR, NF, 8, w1),
            buf(NF, 8, w1), buf(NF, 8, w1), buf(NF, NR, 8, w0), buf(NF, NR, 8, w0),
            buf(8, 128), buf(NF, 8, 128), buf(8, 128), buf(3, 8, 128),
            dma((11,)),
            dma((2, 6)), dma((2, 6)), dma((2,)), dma((2,)), dma((1,)), dma((1,)), dma((1,)), dma((1,)),
            dma((1,)), dma((1,)), dma((2, 6)), dma((2, 6)), dma((6,)), dma((6,)),
            dma((1,)), dma((1,)), dma((1,)), dma((1,)), dma((3,)), dma((3,)),
        ],
        compiler_params=pltpu.CompilerParams(
            collective_id=0, has_side_effects=True, vmem_limit_bytes=43 * 2**20
        ),
        name="outer_step",
    )(
        global_params.reshape(col4), local_params.reshape(col4), flip_signs.reshape(FULL // 128, 128),
        momentum.reshape(row4), stale_codes.reshape(row4), stale_scale,
    )
    new_params, new_momentum, new_stale, new_scale = pl.pallas_call(
        writer,
        out_shape=(shape(col4, F32), shape(row4, F32), shape(row4, F32), shape((1,), F32)),
        in_specs=[vmem] * 4,
        out_specs=(hbm, hbm, hbm, smem),
        scratch_shapes=[buf(*row4), dma((3 * NR,))],
        compiler_params=pltpu.CompilerParams(vmem_limit_bytes=16 * 2**20),
        name="write_results",
    )(*results)
    return (
        new_params.reshape(NF * NR * 8, COLS),
        new_momentum.reshape(NR * 8, FULL),
        new_stale.reshape(NR * 8, FULL),
        new_scale,
    )


def solution(mesh):
    placed = (
        P(None, "fsdp"),
        P("replica", None, "fsdp"),
        P(),
        P("fsdp", None),
        P("fsdp", None),
        P(),
    )
    return jax.shard_map(
        body,
        mesh=mesh,
        in_specs=placed,
        out_specs=(P(None, "fsdp"), P("fsdp", None), P("fsdp", None), P()),
        check_vma=False,
    )
```

```python
import jax
import jax.numpy as jnp
from jax import lax
from jax.experimental import pallas as pl
from jax.experimental.pallas import tpu as pltpu
from jax.sharding import PartitionSpec as P

MESH = pl.DeviceIdType.MESH
F32 = jnp.float32
BF16 = jnp.bfloat16
NF = 32
NR = 4
COLS = 896
FULL = NF * COLS
BLOCK = 4096
NBLK = FULL // BLOCK
PARTS = ((512, 384), (0, 512))
CUT = 1
HALF = (pl.ds(0, NF // 2), pl.ds(NF // 2, NF // 2))
ORDER = (4, 12, 1, 3, 5, 15, 7, 13, 8, 2, 9, 6, 11, 14, 10)
PACKED = [sum(v << (4 * i) for i, v in enumerate(ORDER[5 * k : 5 * k + 5])) for k in range(3)]


def fwht(value):
    width = value.shape[1]
    if width == 128:
        return [value]
    left, right = value[:, : width // 2], value[:, width // 2 :]
    return fwht(left + right) + fwht(left - right)


def kernel(
    glob_in, loc_in, flip_in, mom_in, stale_in, sscale_in,
    npf, mom, rot, top_out,
    glob, pg, signs, flips, stale, xrow, xpart, table,
    r1a, r1b, r2a, r2b, gqb, gra, grb, tsend, trecv, nsend, nrecv, mxs, mxr, mys, myr,
    ld_sem,
    rs_s, rs_r, sp_s, sp_r, sc_s, sc_r, t_s, t_r, gq_s, gq_r, ga_s, ga_r, gb_s, gb_r, ret_s, ret_r, mx_s, mx_r, my_s, my_r,
):
    r, f = lax.axis_index("replica"), lax.axis_index("fsdp")
    fx, fz, fc = f // 8, lax.rem(f // 2, 4), lax.rem(f, 2)
    right, left, far = lax.rem(r + 1, 4), lax.rem(r + 3, 4), lax.rem(r + 2, 4)
    to_right, to_left = (right, f), (left, f)

    def remote(src, dst, ss, rs, dev):
        return pltpu.make_async_remote_copy(
            src_ref=src, dst_ref=dst, send_sem=ss, recv_sem=rs, device_id=dev, device_id_type=MESH
        )

    def lanes(index, width=COLS, off=0):
        return pl.ds(pl.multiple_of(index * COLS + off, 128), width)

    def peers(s, dc):
        word = jnp.where(s < 5, PACKED[0], jnp.where(s < 10, PACKED[1], PACKED[2]))
        code = lax.rem(word >> (4 * lax.rem(s, 5)), 16)
        dx, dz = code // 4, lax.rem(code, 4)
        core = lax.rem(fc + dc, 2)
        to = lax.rem(fx + dx, 4) * 8 + lax.rem(fz + dz, 4) * 2 + core
        frm = lax.rem(fx + 4 - dx, 4) * 8 + lax.rem(fz + 4 - dz, 4) * 2 + core
        return to, frm

    other = f + 1 - 2 * fc

    def each_peer(fn, lo=0, hi=15, core=True):
        def step(s, carry):
            for dc in (0, 1):
                to, frm = peers(s, dc)
                fn(to, frm, 2 * s + dc)
            return carry

        lax.fori_loop(lo, hi, step, 0)
        if core:
            fn(other, other, 30)

    def exchange(src, dst, ss, rs, all_src, all_dst):
        def start(to, frm, i):
            remote(src(to), dst(f), ss, rs, (r, to)).start()

        def wait():
            remote(all_src, all_dst, ss, rs, (r, other)).wait_recv()

        def drain():
            remote(all_src, all_dst, ss, rs, (r, other)).wait_send()

        return start, wait, drain

    most = pl.ds(0, NF - 1)

    order = ((far, 2), (left, 3), (right, 1), (r, 0))
    loads = []
    for i, (c, j) in enumerate(order):
        a = pltpu.make_async_copy(loc_in.at[:, c], pg.at[:, j], ld_sem.at[2 * i])
        b = pltpu.make_async_copy(glob_in.at[:, c], glob.at[:, c], ld_sem.at[2 * i + 1])
        loads.append((a, b))
    ld_stale = pltpu.make_async_copy(stale_in, stale, ld_sem.at[8])
    ld_mom = pltpu.make_async_copy(mom_in, mom, ld_sem.at[9])
    ld_signs = pltpu.make_async_copy(flip_in, signs, ld_sem.at[10])
    for load in loads[0]:
        load.start()

    barrier = pltpu.get_barrier_semaphore()

    for s in (1, 2, 3):
        pl.semaphore_signal(barrier, inc=1, device_id=(lax.rem(r + s, 4), f), device_id_type=MESH)

    def greet(s, carry):
        pl.semaphore_signal(
            barrier, inc=1, device_id=(r, lax.rem(f + s, NF)), device_id_type=MESH
        )
        return carry

    lax.fori_loop(1, NF, greet, 0)

    def difference(i):
        c, j = order[i]
        for load in loads[i]:
            load.wait()

        def diff(t, carry):
            rows = pl.ds(4 * t, 4)
            pg[rows, j] = glob[rows, c] - pg[rows, j]
            return carry

        lax.fori_loop(0, NF // 4, diff, 0, unroll=2)

    for i in (1, 2, 3):
        for load in loads[i]:
            load.start()
    difference(0)
    pl.semaphore_wait(barrier, NF - 1 + NR - 1)

    r1 = (r1a, r1b)
    r2 = (r2a, r2b)
    gr = (gra, grb)

    def cols(p):
        return pl.ds(PARTS[p][0], PARTS[p][1])

    def term(p, half, j):
        return xpart.at[j, half] if p == 0 else pg.at[half, j, :, cols(1)]

    def rs_copies(p):
        lo, hi = HALF
        return (
            remote(term(p, lo, 2), r1[p].at[0], rs_s.at[p, 0], rs_r.at[p, 0], to_right),
            remote(term(p, hi, 2), r1[p].at[1], rs_s.at[p, 1], rs_r.at[p, 1], to_left),
            remote(term(p, hi, 1), r2[p].at[0, hi], rs_s.at[p, 2], rs_r.at[p, 2], to_right),
            remote(term(p, lo, 3), r2[p].at[1, lo], rs_s.at[p, 3], rs_r.at[p, 3], to_left),
            remote(r1[p].at[0], r2[p].at[0, lo], rs_s.at[p, 4], rs_r.at[p, 4], to_right),
            remote(r1[p].at[1], r2[p].at[1, hi], rs_s.at[p, 5], rs_r.at[p, 5], to_left),
        )

    rs = (rs_copies(0), rs_copies(1))

    def rs_second(p):
        for side, j, base in ((0, 1, 0), (1, 3, NF // 2)):
            rs[p][side].wait_recv()

            def add(t, carry, side=side, j=j, base=base):
                rows = pl.ds(4 * t, 4)
                r1[p][side, rows] = r1[p][side, rows] + term(p, pl.ds(base + 4 * t, 4), j)[...]
                return carry

            lax.fori_loop(0, NF // 8, add, 0, unroll=2)
            rs[p][4 + side].start()

    def rs_last(p):
        for i in range(2, 6):
            rs[p][i].wait_recv()

        def add(t, carry):
            rows = pl.ds(4 * t, 4)
            total = term(p, rows, 0)[...] + (r2[p][0, rows] + r2[p][1, rows])
            if p == 0:
                gra[r, rows] = total
            else:
                gqb[rows] = total
            return carry

        lax.fori_loop(0, NF // 4, add, 0, unroll=2)

    for i in (0, 1):
        rs[1][i].start()
    off1, wid1 = PARTS[1]
    off0, wid0 = PARTS[0]
    def sp_exchange(k):
        pair = pl.ds(2 * k, 2)
        return exchange(
            lambda to: pg.at[to, pair, :, cols(0)], lambda frm: xpart.at[pair, frm],
            sp_s.at[k], sp_r.at[k], pg.at[most, pair, :, cols(0)], xpart.at[pair, most],
        )

    sp = (sp_exchange(0), sp_exchange(1))
    sc_start, sc_wait, sc_drain = exchange(
        lambda to: pg.at[to, :, :, cols(1)], lambda frm: xrow.at[:, :, lanes(frm, wid1, off1)],
        sc_s.at[0], sc_r.at[0], pg.at[most, :, :, cols(1)], xrow.at[:, :, pl.ds(0, (NF - 1) * wid1)],
    )
    difference(1)
    rs[1][3].start()
    each_peer(sp[1][0])
    ld_signs.start()
    ld_stale.start()
    ld_mom.start()
    difference(2)
    rs[1][2].start()
    difference(3)
    each_peer(sp[0][0])
    for i in range(NR):
        xpart[i, f] = pg[f, i, :, cols(0)]
        xrow[i, :, lanes(f, wid1, off1)] = pg[f, i, :, cols(1)]

    ld_signs.wait()

    def flip_step(t, carry):
        rows = (2 * signs[pl.ds(8 * t, 8), :] - 1).astype(F32)
        flips[:, pl.ds(pl.multiple_of(t * 1024, 1024), 1024)] = jnp.concatenate(
            [jnp.broadcast_to(rows[i : i + 1], (8, 128)) for i in range(8)], axis=1
        )
        return carry

    lax.fori_loop(0, FULL // 1024, flip_step, 0, unroll=2)
    bits = lax.broadcasted_iota(jnp.int32, (256, 128), 0) & lax.broadcasted_iota(jnp.int32, (256, 128), 1)
    parity = jnp.zeros((256, 128), jnp.int32)
    for b in range(7):
        parity = parity ^ (bits >> b)
    table[...] = jnp.where((parity & 1) == 0, 1.0 / 64.0, -1.0 / 64.0).astype(F32).astype(BF16)

    def hadamard(value):
        x = jnp.concatenate(fwht(value), axis=0)
        high = x.astype(BF16)
        low = (x - high.astype(F32)).astype(BF16)
        return jnp.dot(
            jnp.concatenate([high, low], axis=1), table[...], preferred_element_type=F32
        )

    def to_rows(value):
        return jnp.concatenate([value[8 * a : 8 * a + 8] for a in range(32)], axis=1)

    def blk(k):
        return pl.ds(pl.multiple_of(k * BLOCK, BLOCK), BLOCK)

    coef = 0.5 * (sscale_in[0] / 127.0)
    ld_stale.wait()

    def stale_step(t, carry):
        i, k = t // NBLK, lax.rem(t, NBLK)
        stale[i, :, blk(k)] = to_rows(hadamard(stale[i, :, blk(k)])) * (flips[:, blk(k)] * coef)
        return carry

    lax.fori_loop(0, NR * NBLK, stale_step, 0, unroll=4)
    ld_mom.wait()

    def t_step(g, carry):
        tsend[g] = 1.9 * stale[r, :, lanes(g, wid1, off1)] + 0.81 * mom[r, :, lanes(g, wid1, off1)]
        return carry

    lax.fori_loop(0, NF, t_step, 0, unroll=4)
    t_start, t_wait, t_drain = exchange(
        lambda to: tsend.at[to], lambda frm: trecv.at[frm], t_s.at[0], t_r.at[0],
        tsend.at[most], trecv.at[most],
    )
    each_peer(t_start)
    trecv[f] = tsend[f]

    each_peer(sc_start, 0, CUT, True)

    gq_start, gq_wait, gq_drain = exchange(
        lambda to: gqb.at[to], lambda frm: grb.at[r, frm], gq_s.at[0], gq_r.at[0],
        gqb.at[most], grb.at[r, most],
    )

    def gather(ref, ss, sr):
        return (
            remote(ref(r, 0), ref(r, 0), ss.at[0], sr.at[0], to_right),
            remote(ref(r, 1), ref(r, 1), ss.at[1], sr.at[1], to_left),
            remote(ref(r, 1), ref(r, 1), ss.at[2], sr.at[2], to_right),
            remote(ref(r, 0), ref(r, 0), ss.at[3], sr.at[3], to_left),
            remote(ref(left, 0), ref(left, 0), ss.at[4], sr.at[4], to_right),
            remote(ref(right, 1), ref(right, 1), ss.at[5], sr.at[5], to_left),
        )

    ga = [
        gather(lambda c, h, p=p: gr[p].at[c, HALF[h]], ga_s.at[p], ga_r.at[p]) for p in (0, 1)
    ]
    gb = gather(lambda c, h: npf.at[HALF[h], c, :, cols(1)], gb_s, gb_r)

    def gather_start(g):
        for i in range(4):
            g[i].start()

    def gather_forward(g):
        for i in range(2):
            g[i].wait_recv()
            g[4 + i].start()

    def rows_of(i):
        def mom_step(g, carry):
            for p, (off, wid) in enumerate(PARTS):
                at = lanes(g, wid, off)
                v = gr[p][i, g]
                mom[i, :, at] = 0.9 * mom[i, :, at] + (0.125 * v + stale[i, :, at])
                rot[i, :, at] = v * flips[:, at]
            return carry

        lax.fori_loop(0, NF, mom_step, 0, unroll=4)

        def rot_step(k, carry):
            rot[i, :, blk(k)] = to_rows(hadamard(rot[i, :, blk(k)]))
            return carry

        lax.fori_loop(0, NBLK, rot_step, 0, unroll=NBLK)

    rs_second(1)
    sp[1][1]()
    for i in (0, 1, 3):
        rs[0][i].start()
    sp[0][1]()
    rs[0][2].start()

    def part_step(t, carry):
        i, g = t // NF, lax.rem(t, NF)
        xrow[i, :, lanes(g, wid0, off0)] = xpart[i, g]
        return carry

    lax.fori_loop(0, NR * NF, part_step, 0, unroll=4)

    rs_last(1)
    each_peer(gq_start)
    each_peer(sc_start, CUT, 15, False)
    grb[r, f] = gqb[f]
    t_wait()

    def np_step(t, carry):
        rows = pl.ds(4 * t, 4)
        npf[rows, r, :, cols(1)] = glob[rows, r, :, cols(1)] - 0.7 * (trecv[rows] + 0.2375 * gqb[rows])
        return carry

    lax.fori_loop(0, NF // 4, np_step, 0, unroll=2)
    rs_second(0)
    for i in (0, 1):
        gb[i].start()
    rs_last(0)
    gather_start(ga[0])
    gather_forward(ga[0])
    for i in (2, 3):
        gb[i].start()
    gq_wait()
    gather_start(ga[1])

    for i in range(2, 6):
        ga[0][i].wait_recv()

    def n_step(t, carry):
        i, g = t // NF, lax.rem(t, NF)
        nsend[g, i] = (
            1.9 * (0.125 * gra[i, g] + stale[i, :, lanes(g, wid0, off0)])
            + 0.81 * mom[i, :, lanes(g, wid0, off0)]
        )
        return carry

    lax.fori_loop(0, NR * NF, n_step, 0, unroll=4)
    ret_start, ret_wait, ret_drain = exchange(
        lambda to: nsend.at[to], lambda frm: nrecv.at[frm], ret_s.at[0], ret_r.at[0],
        nsend.at[most], nrecv.at[most],
    )
    each_peer(ret_start, 0, 9, False)
    nrecv[f] = nsend[f]

    rows_of(r)
    sc_wait()

    def scale_step(t, top):
        i, k = t // NBLK, lax.rem(t, NBLK)
        y = jnp.abs(hadamard(xrow[i, :, blk(k)] * flips[:, blk(k)]))
        return jnp.maximum(top, jnp.max(y.reshape(32, 8, 128), axis=0))

    mxs[...] = lax.fori_loop(0, NR * NBLK, scale_step, jnp.zeros((8, 128), F32), unroll=4)
    mx_start, mx_wait, mx_drain = exchange(
        lambda to: mxs, lambda frm: mxr.at[frm], mx_s.at[0], mx_r.at[0], mxr.at[most], mxr.at[most]
    )
    each_peer(mx_start)
    each_peer(ret_start, 9, 15, True)
    mxr[f] = mxs[...]

    gather_forward(ga[1])
    gather_forward(gb)

    ga[1][3].wait_recv()
    rows_of(right)
    ga[1][2].wait_recv()
    rows_of(left)
    mx_wait()
    mys[...] = jnp.max(mxr[...], axis=0)

    def my_copy(s):
        return remote(
            mys, myr.at[s - 1], my_s.at[s - 1], my_r.at[s - 1], (lax.rem(r + s, 4), f)
        )

    for s in (1, 2, 3):
        my_copy(s).start()

    for i in (4, 5):
        ga[1][i].wait_recv()
    rows_of(far)

    ret_wait()

    def np0_step(t, carry):
        npf[t, :, :, cols(0)] = glob[t, :, :, cols(0)] - 0.7 * nrecv[t]
        return carry

    lax.fori_loop(0, NF, np0_step, 0, unroll=4)
    for s in (1, 2, 3):
        my_copy(s).wait_recv()
    top_out[...] = jnp.maximum(jnp.max(myr[...], axis=0), mys[...])
    for i in range(2, 6):
        gb[i].wait_recv()

    for p in (0, 1):
        for c in rs[p]:
            c.wait_send()
        for c in ga[p]:
            c.wait_send()
    for c in gb:
        c.wait_send()
    for d in (sp[0][2], sp[1][2], sc_drain, t_drain, gq_drain, ret_drain, mx_drain):
        d()
    for s in (1, 2, 3):
        my_copy(s).wait_send()


def writer(npf, mom, rot, top, np_out, nm_out, ns_out, sc_out, scaled, sem):
    stores = []
    for i in range(NR):
        rows = pl.ds(8 * i, 8)
        stores.append(pltpu.make_async_copy(npf.at[rows], np_out.at[rows], sem.at[i]))
        stores.append(pltpu.make_async_copy(mom.at[i], nm_out.at[i], sem.at[4 + i]))
    for c in stores:
        c.start()
    scale = jnp.max(top[...]) + 1e-06
    sc_out[0] = scale
    factor = 31.75 / jnp.broadcast_to(scale, (8, 128))
    wide = jnp.concatenate([factor] * (COLS // 128), axis=1)
    for i in range(NR):

        def step(t, carry, i=i):
            at = pl.ds(pl.multiple_of(t * COLS, 128), COLS)
            scaled[i, :, at] = rot[i, :, at] * wide
            return carry

        lax.fori_loop(0, NF, step, 0, unroll=4)
        stores.append(pltpu.make_async_copy(scaled.at[i], ns_out.at[i], sem.at[8 + i]))
        stores[-1].start()
    for c in stores:
        c.wait()


def body(global_params, local_params, flip_signs, momentum, stale_codes, stale_scale):
    shape = jax.ShapeDtypeStruct
    hbm = pl.BlockSpec(memory_space=pltpu.HBM)
    vmem = pl.BlockSpec(memory_space=pltpu.VMEM)
    smem = pl.BlockSpec(memory_space=pltpu.SMEM)
    dma = pltpu.SemaphoreType.DMA
    w0, w1 = PARTS[0][1], PARTS[1][1]
    col4, row4 = (NF, NR, 8, COLS), (NR, 8, FULL)

    def buf(*dims):
        return pltpu.VMEM(dims, F32)

    results = pl.pallas_call(
        kernel,
        out_shape=(shape(col4, F32), shape(row4, F32), shape(row4, F32), shape((8, 128), F32)),
        in_specs=[hbm, hbm, hbm, hbm, hbm, smem],
        out_specs=(vmem, vmem, vmem, vmem),
        scratch_shapes=[
            buf(*col4), buf(*col4), pltpu.VMEM((FULL // 128, 128), jnp.int32), buf(8, FULL), buf(*row4), buf(*row4),
            buf(NR, NF, 8, w0), pltpu.VMEM((256, 128), BF16),
            buf(2, NF // 2, 8, w0), buf(2, NF // 2, 8, w1), buf(2, NF, 8, w0), buf(2, NF, 8, w1),
            buf(NF, 8, w1), buf(NR, NF, 8, w0), buf(NR, NF, 8, w1),
            buf(NF, 8, w1), buf(NF, 8, w1), buf(NF, NR, 8, w0), buf(NF, NR, 8, w0),
            buf(8, 128), buf(NF, 8, 128), buf(8, 128), buf(3, 8, 128),
            dma((11,)),
            dma((2, 6)), dma((2, 6)), dma((2,)), dma((2,)), dma((1,)), dma((1,)), dma((1,)), dma((1,)),
            dma((1,)), dma((1,)), dma((2, 6)), dma((2, 6)), dma((6,)), dma((6,)),
            dma((1,)), dma((1,)), dma((1,)), dma((1,)), dma((3,)), dma((3,)),
        ],
        compiler_params=pltpu.CompilerParams(
            collective_id=0, has_side_effects=True, vmem_limit_bytes=43 * 2**20
        ),
        name="outer_step",
    )(
        global_params.reshape(col4), local_params.reshape(col4), flip_signs.reshape(FULL // 128, 128),
        momentum.reshape(row4), stale_codes.reshape(row4), stale_scale,
    )
    new_params, new_momentum, new_stale, new_scale = pl.pallas_call(
        writer,
        out_shape=(shape(col4, F32), shape(row4, F32), shape(row4, F32), shape((1,), F32)),
        in_specs=[vmem] * 4,
        out_specs=(hbm, hbm, hbm, smem),
        scratch_shapes=[buf(*row4), dma((3 * NR,))],
        compiler_params=pltpu.CompilerParams(vmem_limit_bytes=16 * 2**20),
        name="write_results",
    )(*results)
    return (
        new_params.reshape(NF * NR * 8, COLS),
        new_momentum.reshape(NR * 8, FULL),
        new_stale.reshape(NR * 8, FULL),
        new_scale,
    )


def solution(mesh):
    placed = (
        P(None, "fsdp"),
        P("replica", None, "fsdp"),
        P(),
        P("fsdp", None),
        P("fsdp", None),
        P(),
    )
    return jax.shard_map(
        body,
        mesh=mesh,
        in_specs=placed,
        out_specs=(P(None, "fsdp"), P("fsdp", None), P("fsdp", None), P()),
        check_vma=False,
    )
```

```python
import jax
import jax.numpy as jnp
from jax import lax
from jax.experimental import pallas as pl
from jax.experimental.pallas import tpu as pltpu
from jax.sharding import PartitionSpec as P

MESH = pl.DeviceIdType.MESH
F32 = jnp.float32
BF16 = jnp.bfloat16
NF = 32
NR = 4
COLS = 896
FULL = NF * COLS
BLOCK = 4096
NBLK = FULL // BLOCK
PARTS = ((512, 384), (0, 512))
CUT = 1
HALF = (pl.ds(0, NF // 2), pl.ds(NF // 2, NF // 2))
ORDER = (4, 12, 1, 3, 5, 15, 7, 13, 8, 2, 9, 6, 11, 14, 10)
PACKED = [sum(v << (4 * i) for i, v in enumerate(ORDER[5 * k : 5 * k + 5])) for k in range(3)]


def fwht(value):
    width = value.shape[1]
    if width == 128:
        return [value]
    left, right = value[:, : width // 2], value[:, width // 2 :]
    return fwht(left + right) + fwht(left - right)


def kernel(
    glob_in, loc_in, flip_in, mom_in, stale_in, sscale_in,
    npf, mom, rot, top_out,
    glob, pg, signs, flips, stale, xrow, xpart, table,
    r1a, r1b, r2a, r2b, gqb, gra, grb, tsend, trecv, nsend, nrecv, mxs, mxr, mys, myr,
    ld_sem,
    rs_s, rs_r, sp_s, sp_r, sc_s, sc_r, t_s, t_r, gq_s, gq_r, ga_s, ga_r, gb_s, gb_r, ret_s, ret_r, mx_s, mx_r, my_s, my_r,
):
    r, f = lax.axis_index("replica"), lax.axis_index("fsdp")
    fx, fz, fc = f // 8, lax.rem(f // 2, 4), lax.rem(f, 2)
    right, left, far = lax.rem(r + 1, 4), lax.rem(r + 3, 4), lax.rem(r + 2, 4)
    to_right, to_left = (right, f), (left, f)

    def remote(src, dst, ss, rs, dev):
        return pltpu.make_async_remote_copy(
            src_ref=src, dst_ref=dst, send_sem=ss, recv_sem=rs, device_id=dev, device_id_type=MESH
        )

    def lanes(index, width=COLS, off=0):
        return pl.ds(pl.multiple_of(index * COLS + off, 128), width)

    def peers(s, dc):
        word = jnp.where(s < 5, PACKED[0], jnp.where(s < 10, PACKED[1], PACKED[2]))
        code = lax.rem(word >> (4 * lax.rem(s, 5)), 16)
        dx, dz = code // 4, lax.rem(code, 4)
        core = lax.rem(fc + dc, 2)
        to = lax.rem(fx + dx, 4) * 8 + lax.rem(fz + dz, 4) * 2 + core
        frm = lax.rem(fx + 4 - dx, 4) * 8 + lax.rem(fz + 4 - dz, 4) * 2 + core
        return to, frm

    other = f + 1 - 2 * fc

    def each_peer(fn, lo=0, hi=15, core=True):
        def step(s, carry):
            for dc in (0, 1):
                to, frm = peers(s, dc)
                fn(to, frm, 2 * s + dc)
            return carry

        lax.fori_loop(lo, hi, step, 0)
        if core:
            fn(other, other, 30)

    def exchange(src, dst, ss, rs, all_src, all_dst):
        def start(to, frm, i):
            remote(src(to), dst(f), ss, rs, (r, to)).start()

        def wait():
            remote(all_src, all_dst, ss, rs, (r, other)).wait_recv()

        def drain():
            remote(all_src, all_dst, ss, rs, (r, other)).wait_send()

        return start, wait, drain

    most = pl.ds(0, NF - 1)

    order = ((far, 2), (left, 3), (right, 1), (r, 0))
    loads = []
    for i, (c, j) in enumerate(order):
        a = pltpu.make_async_copy(loc_in.at[:, c], pg.at[:, j], ld_sem.at[2 * i])
        b = pltpu.make_async_copy(glob_in.at[:, c], glob.at[:, c], ld_sem.at[2 * i + 1])
        loads.append((a, b))
    ld_stale = pltpu.make_async_copy(stale_in, stale, ld_sem.at[8])
    ld_mom = pltpu.make_async_copy(mom_in, mom, ld_sem.at[9])
    ld_signs = pltpu.make_async_copy(flip_in, signs, ld_sem.at[10])
    for load in loads[0]:
        load.start()

    barrier = pltpu.get_barrier_semaphore()

    for s in (1, 2, 3):
        pl.semaphore_signal(barrier, inc=1, device_id=(lax.rem(r + s, 4), f), device_id_type=MESH)

    def greet(s, carry):
        pl.semaphore_signal(
            barrier, inc=1, device_id=(r, lax.rem(f + s, NF)), device_id_type=MESH
        )
        return carry

    lax.fori_loop(1, NF, greet, 0)

    def difference(i):
        c, j = order[i]
        for load in loads[i]:
            load.wait()

        def diff(t, carry):
            rows = pl.ds(4 * t, 4)
            pg[rows, j] = glob[rows, c] - pg[rows, j]
            return carry

        lax.fori_loop(0, NF // 4, diff, 0, unroll=2)

    for load in loads[1]:
        load.start()
    difference(0)
    for i in (2, 3):
        for load in loads[i]:
            load.start()
    pl.semaphore_wait(barrier, NF - 1 + NR - 1)

    r1 = (r1a, r1b)
    r2 = (r2a, r2b)
    gr = (gra, grb)

    def cols(p):
        return pl.ds(PARTS[p][0], PARTS[p][1])

    def term(p, half, j):
        return xpart.at[j, half] if p == 0 else pg.at[half, j, :, cols(1)]

    def rs_copies(p):
        lo, hi = HALF
        return (
            remote(term(p, lo, 2), r1[p].at[0], rs_s.at[p, 0], rs_r.at[p, 0], to_right),
            remote(term(p, hi, 2), r1[p].at[1], rs_s.at[p, 1], rs_r.at[p, 1], to_left),
            remote(term(p, hi, 1), r2[p].at[0, hi], rs_s.at[p, 2], rs_r.at[p, 2], to_right),
            remote(term(p, lo, 3), r2[p].at[1, lo], rs_s.at[p, 3], rs_r.at[p, 3], to_left),
            remote(r1[p].at[0], r2[p].at[0, lo], rs_s.at[p, 4], rs_r.at[p, 4], to_right),
            remote(r1[p].at[1], r2[p].at[1, hi], rs_s.at[p, 5], rs_r.at[p, 5], to_left),
        )

    rs = (rs_copies(0), rs_copies(1))

    def rs_second(p):
        for side, j, base in ((0, 1, 0), (1, 3, NF // 2)):
            rs[p][side].wait_recv()

            def add(t, carry, side=side, j=j, base=base):
                rows = pl.ds(4 * t, 4)
                r1[p][side, rows] = r1[p][side, rows] + term(p, pl.ds(base + 4 * t, 4), j)[...]
                return carry

            lax.fori_loop(0, NF // 8, add, 0, unroll=2)
            rs[p][4 + side].start()

    def rs_last(p):
        for i in range(2, 6):
            rs[p][i].wait_recv()

        def add(t, carry):
            rows = pl.ds(4 * t, 4)
            total = term(p, rows, 0)[...] + (r2[p][0, rows] + r2[p][1, rows])
            if p == 0:
                gra[r, rows] = total
            else:
                gqb[rows] = total
            return carry

        lax.fori_loop(0, NF // 4, add, 0, unroll=2)

    for i in (0, 1):
        rs[1][i].start()
    off1, wid1 = PARTS[1]
    off0, wid0 = PARTS[0]
    def sp_exchange(k):
        pair = pl.ds(2 * k, 2)
        return exchange(
            lambda to: pg.at[to, pair, :, cols(0)], lambda frm: xpart.at[pair, frm],
            sp_s.at[k], sp_r.at[k], pg.at[most, pair, :, cols(0)], xpart.at[pair, most],
        )

    sp = (sp_exchange(0), sp_exchange(1))
    sc_start, sc_wait, sc_drain = exchange(
        lambda to: pg.at[to, :, :, cols(1)], lambda frm: xrow.at[:, :, lanes(frm, wid1, off1)],
        sc_s.at[0], sc_r.at[0], pg.at[most, :, :, cols(1)], xrow.at[:, :, pl.ds(0, (NF - 1) * wid1)],
    )
    difference(1)
    rs[1][3].start()
    each_peer(sp[1][0])
    ld_signs.start()
    ld_stale.start()
    ld_mom.start()
    difference(2)
    rs[1][2].start()
    difference(3)
    each_peer(sp[0][0])
    for i in range(NR):
        xpart[i, f] = pg[f, i, :, cols(0)]
        xrow[i, :, lanes(f, wid1, off1)] = pg[f, i, :, cols(1)]

    ld_signs.wait()

    def flip_step(t, carry):
        rows = (2 * signs[pl.ds(8 * t, 8), :] - 1).astype(F32)
        flips[:, pl.ds(pl.multiple_of(t * 1024, 1024), 1024)] = jnp.concatenate(
            [jnp.broadcast_to(rows[i : i + 1], (8, 128)) for i in range(8)], axis=1
        )
        return carry

    lax.fori_loop(0, FULL // 1024, flip_step, 0, unroll=2)
    bits = lax.broadcasted_iota(jnp.int32, (256, 128), 0) & lax.broadcasted_iota(jnp.int32, (256, 128), 1)
    parity = jnp.zeros((256, 128), jnp.int32)
    for b in range(7):
        parity = parity ^ (bits >> b)
    table[...] = jnp.where((parity & 1) == 0, 1.0 / 64.0, -1.0 / 64.0).astype(F32).astype(BF16)

    def hadamard(value):
        x = jnp.concatenate(fwht(value), axis=0)
        high = x.astype(BF16)
        low = (x - high.astype(F32)).astype(BF16)
        return jnp.dot(
            jnp.concatenate([high, low], axis=1), table[...], preferred_element_type=F32
        )

    def to_rows(value):
        return jnp.concatenate([value[8 * a : 8 * a + 8] for a in range(32)], axis=1)

    def blk(k):
        return pl.ds(pl.multiple_of(k * BLOCK, BLOCK), BLOCK)

    coef = 0.5 * (sscale_in[0] / 127.0)
    ld_stale.wait()

    def stale_step(t, carry):
        i, k = t // NBLK, lax.rem(t, NBLK)
        stale[i, :, blk(k)] = to_rows(hadamard(stale[i, :, blk(k)])) * (flips[:, blk(k)] * coef)
        return carry

    lax.fori_loop(0, NR * NBLK, stale_step, 0, unroll=4)
    ld_mom.wait()

    def t_step(g, carry):
        tsend[g] = 1.9 * stale[r, :, lanes(g, wid1, off1)] + 0.81 * mom[r, :, lanes(g, wid1, off1)]
        return carry

    lax.fori_loop(0, NF, t_step, 0, unroll=4)
    t_start, t_wait, t_drain = exchange(
        lambda to: tsend.at[to], lambda frm: trecv.at[frm], t_s.at[0], t_r.at[0],
        tsend.at[most], trecv.at[most],
    )
    each_peer(t_start)
    trecv[f] = tsend[f]

    each_peer(sc_start, 0, CUT, True)

    gq_start, gq_wait, gq_drain = exchange(
        lambda to: gqb.at[to], lambda frm: grb.at[r, frm], gq_s.at[0], gq_r.at[0],
        gqb.at[most], grb.at[r, most],
    )

    def gather(ref, ss, sr):
        return (
            remote(ref(r, 0), ref(r, 0), ss.at[0], sr.at[0], to_right),
            remote(ref(r, 1), ref(r, 1), ss.at[1], sr.at[1], to_left),
            remote(ref(r, 1), ref(r, 1), ss.at[2], sr.at[2], to_right),
            remote(ref(r, 0), ref(r, 0), ss.at[3], sr.at[3], to_left),
            remote(ref(left, 0), ref(left, 0), ss.at[4], sr.at[4], to_right),
            remote(ref(right, 1), ref(right, 1), ss.at[5], sr.at[5], to_left),
        )

    ga = [
        gather(lambda c, h, p=p: gr[p].at[c, HALF[h]], ga_s.at[p], ga_r.at[p]) for p in (0, 1)
    ]
    gb = gather(lambda c, h: npf.at[HALF[h], c, :, cols(1)], gb_s, gb_r)

    def gather_start(g):
        for i in range(4):
            g[i].start()

    def gather_forward(g):
        for i in range(2):
            g[i].wait_recv()
            g[4 + i].start()

    def rows_of(i):
        def mom_step(g, carry):
            for p, (off, wid) in enumerate(PARTS):
                at = lanes(g, wid, off)
                v = gr[p][i, g]
                mom[i, :, at] = 0.9 * mom[i, :, at] + (0.125 * v + stale[i, :, at])
                rot[i, :, at] = v * flips[:, at]
            return carry

        lax.fori_loop(0, NF, mom_step, 0, unroll=4)

        def rot_step(k, carry):
            rot[i, :, blk(k)] = to_rows(hadamard(rot[i, :, blk(k)]))
            return carry

        lax.fori_loop(0, NBLK, rot_step, 0, unroll=NBLK)

    rs_second(1)
    sp[1][1]()
    for i in (0, 1, 3):
        rs[0][i].start()
    sp[0][1]()
    rs[0][2].start()

    def part_step(t, carry):
        i, g = t // NF, lax.rem(t, NF)
        xrow[i, :, lanes(g, wid0, off0)] = xpart[i, g]
        return carry

    lax.fori_loop(0, NR * NF, part_step, 0, unroll=4)

    rs_last(1)
    each_peer(gq_start)
    each_peer(sc_start, CUT, 15, False)
    grb[r, f] = gqb[f]
    t_wait()

    def np_step(t, carry):
        rows = pl.ds(4 * t, 4)
        npf[rows, r, :, cols(1)] = glob[rows, r, :, cols(1)] - 0.7 * (trecv[rows] + 0.2375 * gqb[rows])
        return carry

    lax.fori_loop(0, NF // 4, np_step, 0, unroll=2)
    rs_second(0)
    for i in (0, 1):
        gb[i].start()
    rs_last(0)
    gather_start(ga[0])
    gather_forward(ga[0])
    for i in (2, 3):
        gb[i].start()
    gq_wait()
    gather_start(ga[1])

    for i in range(2, 6):
        ga[0][i].wait_recv()

    def n_step(t, carry):
        i, g = t // NF, lax.rem(t, NF)
        nsend[g, i] = (
            1.9 * (0.125 * gra[i, g] + stale[i, :, lanes(g, wid0, off0)])
            + 0.81 * mom[i, :, lanes(g, wid0, off0)]
        )
        return carry

    lax.fori_loop(0, NR * NF, n_step, 0, unroll=4)
    ret_start, ret_wait, ret_drain = exchange(
        lambda to: nsend.at[to], lambda frm: nrecv.at[frm], ret_s.at[0], ret_r.at[0],
        nsend.at[most], nrecv.at[most],
    )
    each_peer(ret_start, 0, 9, False)
    nrecv[f] = nsend[f]

    rows_of(r)
    sc_wait()

    def scale_step(t, top):
        i, k = t // NBLK, lax.rem(t, NBLK)
        y = jnp.abs(hadamard(xrow[i, :, blk(k)] * flips[:, blk(k)]))
        return jnp.maximum(top, jnp.max(y.reshape(32, 8, 128), axis=0))

    mxs[...] = lax.fori_loop(0, NR * NBLK, scale_step, jnp.zeros((8, 128), F32), unroll=4)
    mx_start, mx_wait, mx_drain = exchange(
        lambda to: mxs, lambda frm: mxr.at[frm], mx_s.at[0], mx_r.at[0], mxr.at[most], mxr.at[most]
    )
    each_peer(mx_start)
    each_peer(ret_start, 9, 15, True)
    mxr[f] = mxs[...]

    gather_forward(ga[1])
    gather_forward(gb)

    ga[1][3].wait_recv()
    rows_of(right)
    ga[1][2].wait_recv()
    rows_of(left)
    mx_wait()
    mys[...] = jnp.max(mxr[...], axis=0)

    def my_copy(s):
        return remote(
            mys, myr.at[s - 1], my_s.at[s - 1], my_r.at[s - 1], (lax.rem(r + s, 4), f)
        )

    for s in (1, 2, 3):
        my_copy(s).start()

    for i in (4, 5):
        ga[1][i].wait_recv()
    rows_of(far)

    ret_wait()

    def np0_step(t, carry):
        npf[t, :, :, cols(0)] = glob[t, :, :, cols(0)] - 0.7 * nrecv[t]
        return carry

    lax.fori_loop(0, NF, np0_step, 0, unroll=4)
    for s in (1, 2, 3):
        my_copy(s).wait_recv()
    top_out[...] = jnp.maximum(jnp.max(myr[...], axis=0), mys[...])
    for i in range(2, 6):
        gb[i].wait_recv()

    for p in (0, 1):
        for c in rs[p]:
            c.wait_send()
        for c in ga[p]:
            c.wait_send()
    for c in gb:
        c.wait_send()
    for d in (sp[0][2], sp[1][2], sc_drain, t_drain, gq_drain, ret_drain, mx_drain):
        d()
    for s in (1, 2, 3):
        my_copy(s).wait_send()


def writer(npf, mom, rot, top, np_out, nm_out, ns_out, sc_out, scaled, sem):
    stores = []
    for i in range(NR):
        rows = pl.ds(8 * i, 8)
        stores.append(pltpu.make_async_copy(npf.at[rows], np_out.at[rows], sem.at[i]))
        stores.append(pltpu.make_async_copy(mom.at[i], nm_out.at[i], sem.at[4 + i]))
    for c in stores:
        c.start()
    scale = jnp.max(top[...]) + 1e-06
    sc_out[0] = scale
    factor = 31.75 / jnp.broadcast_to(scale, (8, 128))
    wide = jnp.concatenate([factor] * (COLS // 128), axis=1)
    for i in range(NR):

        def step(t, carry, i=i):
            at = pl.ds(pl.multiple_of(t * COLS, 128), COLS)
            scaled[i, :, at] = rot[i, :, at] * wide
            return carry

        lax.fori_loop(0, NF, step, 0, unroll=4)
        stores.append(pltpu.make_async_copy(scaled.at[i], ns_out.at[i], sem.at[8 + i]))
        stores[-1].start()
    for c in stores:
        c.wait()


def body(global_params, local_params, flip_signs, momentum, stale_codes, stale_scale):
    shape = jax.ShapeDtypeStruct
    hbm = pl.BlockSpec(memory_space=pltpu.HBM)
    vmem = pl.BlockSpec(memory_space=pltpu.VMEM)
    smem = pl.BlockSpec(memory_space=pltpu.SMEM)
    dma = pltpu.SemaphoreType.DMA
    w0, w1 = PARTS[0][1], PARTS[1][1]
    col4, row4 = (NF, NR, 8, COLS), (NR, 8, FULL)

    def buf(*dims):
        return pltpu.VMEM(dims, F32)

    results = pl.pallas_call(
        kernel,
        out_shape=(shape(col4, F32), shape(row4, F32), shape(row4, F32), shape((8, 128), F32)),
        in_specs=[hbm, hbm, hbm, hbm, hbm, smem],
        out_specs=(vmem, vmem, vmem, vmem),
        scratch_shapes=[
            buf(*col4), buf(*col4), pltpu.VMEM((FULL // 128, 128), jnp.int32), buf(8, FULL), buf(*row4), buf(*row4),
            buf(NR, NF, 8, w0), pltpu.VMEM((256, 128), BF16),
            buf(2, NF // 2, 8, w0), buf(2, NF // 2, 8, w1), buf(2, NF, 8, w0), buf(2, NF, 8, w1),
            buf(NF, 8, w1), buf(NR, NF, 8, w0), buf(NR, NF, 8, w1),
            buf(NF, 8, w1), buf(NF, 8, w1), buf(NF, NR, 8, w0), buf(NF, NR, 8, w0),
            buf(8, 128), buf(NF, 8, 128), buf(8, 128), buf(3, 8, 128),
            dma((11,)),
            dma((2, 6)), dma((2, 6)), dma((2,)), dma((2,)), dma((1,)), dma((1,)), dma((1,)), dma((1,)),
            dma((1,)), dma((1,)), dma((2, 6)), dma((2, 6)), dma((6,)), dma((6,)),
            dma((1,)), dma((1,)), dma((1,)), dma((1,)), dma((3,)), dma((3,)),
        ],
        compiler_params=pltpu.CompilerParams(
            collective_id=0, has_side_effects=True, vmem_limit_bytes=43 * 2**20
        ),
        name="outer_step",
    )(
        global_params.reshape(col4), local_params.reshape(col4), flip_signs.reshape(FULL // 128, 128),
        momentum.reshape(row4), stale_codes.reshape(row4), stale_scale,
    )
    new_params, new_momentum, new_stale, new_scale = pl.pallas_call(
        writer,
        out_shape=(shape(col4, F32), shape(row4, F32), shape(row4, F32), shape((1,), F32)),
        in_specs=[vmem] * 4,
        out_specs=(hbm, hbm, hbm, smem),
        scratch_shapes=[buf(*row4), dma((3 * NR,))],
        compiler_params=pltpu.CompilerParams(vmem_limit_bytes=16 * 2**20),
        name="write_results",
    )(*results)
    return (
        new_params.reshape(NF * NR * 8, COLS),
        new_momentum.reshape(NR * 8, FULL),
        new_stale.reshape(NR * 8, FULL),
        new_scale,
    )


def solution(mesh):
    placed = (
        P(None, "fsdp"),
        P("replica", None, "fsdp"),
        P(),
        P("fsdp", None),
        P("fsdp", None),
        P(),
    )
    return jax.shard_map(
        body,
        mesh=mesh,
        in_specs=placed,
        out_specs=(P(None, "fsdp"), P("fsdp", None), P("fsdp", None), P()),
        check_vma=False,
    )
```
